256 devices in a mesh: attn: 16 (over z, core), egrp: 4 (over x), etp: 4 (over y).
Axes of the slice: x: 4, y: 4, z: 8, core: 2. Of those that a mesh axis runs over, the one named last changes fastest.
Arguments:
- queries: bfloat16 [512, 6144], P(('attn', 'egrp'), 'etp'), may hold values from -100 to 100
- cache_keys: bfloat16 [512, 512, 1024], P(('attn', 'egrp'), None, 'etp'), may hold values from -5 to 5
- stored_values: bfloat16 [512, 512, 1024], P(('attn', 'egrp'), None, 'etp'), may hold values from -6 to 6
- lengths: int32 [512], P(('attn', 'egrp')), may hold values from 2 to 512, as said below
- residual_in: bfloat16 [512, 6144], P(('attn', 'egrp'), 'etp'), may hold values from -25 to 25
- norm_gain: bfloat16 [6144], replicated, may hold values from 0.25 to 1.75
- expert_ids: int32 [512, 4], P(('attn', 'egrp')), may hold values from 0 to 7, all different within a row; in each aligned block of 512 rows (0 to 511, 512 to 1023, ...) at most 384 rows name the same one
- expert_scores: float32 [512, 4], P(('attn', 'egrp')), may hold values from 0.05 to 1
- w_gate: bfloat16 [8, 6144, 5376], P('egrp', 'etp', 'attn'), may hold values from -0.078125 to 0.078125
- w_up: bfloat16 [8, 6144, 5376], P('egrp', 'etp', 'attn'), may hold values from -0.078125 to 0.078125
- w_down: bfloat16 [8, 5376, 6144], P('egrp', 'attn', 'etp'), may hold values from -0.078125 to 0.078125
Outputs:
- residual: bfloat16 [512, 6144], P(('attn', 'egrp'), 'etp')
- expert_mix: bfloat16 [512, 6144], P(('attn', 'egrp'), 'etp')
The draws below stay inside these ranges and needn't reach their ends.
Inputs may be any that keep to these rules, and one draw needn't show every extreme that they name: `expert_ids`: each row names 4 different experts; no expert is named by more than 384 rows, a bound that some block reaches. `lengths`: some row's cache is full in every draw.
All inputs are finite; a program needn't handle non-finite values.
Results may differ from the reference program's by a relative error of at most 0.018.
Values may be sent and summed in bfloat16 or wider, within the bound.
No kernel may reach another device: no remote copies, remote signals or barrier semaphores. Data moves between devices by JAX's collectives and lax.ppermute only.
A program may use at most 64 MiB of HBM per device.

```python
import math
import jax
import jax.numpy as jnp
import numpy as np
from jax import lax

D = 6144
QUERY_HEADS = 48
KEY_VALUE_HEADS = 8
HEAD_SIZE = 128
FF = 5376
EXPERTS = 8
TOP = 4
CACHE_POSITIONS = 512
DECODE_ROWS = 512


def draw_queries(key, part):
    key = jax.random.fold_in(key, 3)
    array_shape = (DECODE_ROWS, KEY_VALUE_HEADS, QUERY_HEADS // KEY_VALUE_HEADS, HEAD_SIZE)
    sampled_inputs = jnp.clip(jax.random.normal(key, array_shape, jnp.float32), -5.0, 5.0)
    return sampled_inputs.reshape(DECODE_ROWS, QUERY_HEADS * HEAD_SIZE).astype(jnp.bfloat16)


def draw_cache_keys(key, part):
    key = jax.random.fold_in(key, 5)
    sampled_inputs = jnp.clip(jax.random.normal(key, (DECODE_ROWS, CACHE_POSITIONS, KEY_VALUE_HEADS, HEAD_SIZE), jnp.float32), -5.0, 5.0)
    return sampled_inputs.reshape(DECODE_ROWS, CACHE_POSITIONS, KEY_VALUE_HEADS * HEAD_SIZE).astype(jnp.bfloat16)


def draw_lengths(key, part):
    key = jax.random.fold_in(key, 11)
    leading_keys, key_second = jax.random.split(key)
    first_len = jax.random.randint(leading_keys, (DECODE_ROWS,), 2, CACHE_POSITIONS + 1)
    second_len = jax.random.randint(key_second, (DECODE_ROWS,), 2, CACHE_POSITIONS + 1)
    sampled_inputs = jnp.minimum(first_len, second_len)
    return sampled_inputs.at[0].set(CACHE_POSITIONS).astype(jnp.int32)


def draw_residual_in(key, part):
    key = jax.random.fold_in(key, 7)
    key_rows, key_cols, key_body = jax.random.split(key, 3)
    row_scale = jnp.exp(jax.random.uniform(key_rows, (DECODE_ROWS, 1), jnp.float32, 0.0, 1.1513))
    col_scale = jnp.exp(jax.random.uniform(key_cols, (1, D), jnp.float32, 0.0, 1.1513))
    base_draw = jnp.clip(jax.random.normal(key_body, (DECODE_ROWS, D), jnp.float32), -5.0, 5.0)
    return (0.5 * base_draw * row_scale * col_scale).astype(jnp.bfloat16)


def level_of(stream_key, dims, cuts, low, top_value):
    loudness, own = 1.0, jax.random.fold_in(stream_key, 6)
    for dim, shards_of in cuts:
        steps = jnp.exp(jax.random.uniform(jax.random.fold_in(own, dim), (shards_of,), jnp.float32, low / len(cuts), top_value / len(cuts)))
        loudness = loudness * jnp.repeat(steps, dims[dim] // shards_of).reshape([-1 if axis == dim else 1 for axis in range(len(dims))])
    return loudness


def shared_out(own_key, own, number, rows, number_of, top, most, lean):
    order = jax.random.permutation(own_key, number_of)
    heavy_load, usual = load_shares(number_of, rows * top, most, lean, True), load_shares(number_of, rows * top, most, lean, False)
    places = jnp.arange(number_of)

    def named(sizes, offset_by):
        used = int((sizes > 0).sum())
        fixed = max(1, used // 4)
        passed = fixed + (places - fixed + offset_by * (used - fixed)) % max(1, number_of - fixed)
        return jnp.zeros((number_of,), jnp.int32).at[order[jnp.where(places < fixed, places, passed)]].set(jnp.asarray(sizes, jnp.int32))

    sizes = jnp.where(number % 4 == 0, named(heavy_load, number // 4), named(usual, number - number // 4 - 1))
    mixed = jax.random.permutation(jax.random.fold_in(own, 3), number_of)
    giver, sink = mixed[0:number_of // 2 * 2:2], mixed[1:number_of // 2 * 2:2]
    margin = jnp.minimum(sizes[giver] - 1, most - sizes[sink]) // 2
    margin = jnp.where((giver == order[0]) | (sink == order[0]) | (sizes[sink] == 0), 0, jnp.maximum(margin, 0))
    passed = jax.random.randint(jax.random.fold_in(own, 4), (number_of // 2,), 0, 1 << 20) % (margin + 1)
    sizes = sizes.at[giver].add(-passed).at[sink].add(passed)
    items = jnp.searchsorted(jnp.cumsum(sizes), jnp.arange(rows * top), side="right").astype(jnp.int32)
    table = items.reshape(top, rows).T
    table = table[jax.random.permutation(jax.random.fold_in(own, 1), rows)]
    offset_by = jax.random.randint(jax.random.fold_in(own, 2), (rows, 1), 0, top)
    return jnp.take_along_axis(table, (jnp.arange(top)[None, :] + offset_by) % top, axis=1)


def load_shares(amount, total, limit, slope, full):
    loads = [(1 << 20) // math.isqrt(grade ** slope) + 1 for grade in range(1, amount + 1)]
    largest = limit if full else min(limit, max(-(-total // amount), total * loads[0] // sum(loads)))
    least = 1 if total - largest >= amount - 1 else 0
    counts, spare = [largest] + [least] * (amount - 1), total - largest - least * (amount - 1)
    while spare > 0:
        movable = [i for i in range(1, amount) if counts[i] < largest] or [i for i in range(1, amount) if counts[i] < limit]
        pool, remaining = sum([loads[i] for i in movable]), spare
        for i in movable:
            extra = min(limit - counts[i], max(1, remaining * loads[i] // pool), spare)
            counts[i] = counts[i] + extra
            spare = spare - extra
    return np.array(counts)


def scatter_about(rng, extent, scale, limit, shards=(), kind=jnp.bfloat16):
    result = jax.random.normal(rng, extent, jnp.float32) * scale
    if len(shards) > 0:
        result = level_of(rng, extent, shards, -0.22, 0.18) * result
    return jnp.clip(result, min=-limit, max=limit).astype(kind)


def setup_inputs(seed: int = 0) -> dict:
    streams_of = jax.random.split(jax.random.key(seed), 12)
    queries = draw_queries(jax.random.fold_in(streams_of[11], 71), 0)
    cache_keys = draw_cache_keys(jax.random.fold_in(streams_of[11], 71), 0)
    stored_values = scatter_about(streams_of[2], (DECODE_ROWS, CACHE_POSITIONS, KEY_VALUE_HEADS * HEAD_SIZE), 1.0, 6.0, ((0, 64), (2, 4)))
    lengths = draw_lengths(jax.random.fold_in(streams_of[11], 71), 0)
    residual_in = draw_residual_in(jax.random.fold_in(streams_of[11], 71), 0)
    norm_gain = jnp.clip(1.0 + 0.15 * jax.random.normal(streams_of[5], (D,), jnp.float32), 0.25, 1.75).astype(jnp.bfloat16)
    expert_ids_keys = jax.random.split(jax.random.fold_in(streams_of[6], 1), DECODE_ROWS // DECODE_ROWS)
    expert_ids_turns = jax.random.permutation(jax.random.fold_in(streams_of[6], 3), DECODE_ROWS // DECODE_ROWS)
    expert_ids = jax.vmap(lambda own, number: shared_out(jax.random.fold_in(streams_of[6], 2), own, number, DECODE_ROWS, EXPERTS, TOP, DECODE_ROWS * 3 // 4, 2))(expert_ids_keys, expert_ids_turns).reshape((DECODE_ROWS, TOP))
    expert_scores = jnp.clip(jnp.exp(math.log(1.0) - 2.9957323 * jax.random.uniform(streams_of[7], (DECODE_ROWS, TOP), jnp.float32) ** level_of(streams_of[7], (DECODE_ROWS, TOP), ((0, 64),), -0.2, 0.2)), 0.05, 1.0)
    w_gate = scatter_about(streams_of[8], (EXPERTS, D, FF), D ** -0.5, 0.078125, ((0, 4), (1, 4), (2, 16)))
    w_up = scatter_about(streams_of[9], (EXPERTS, D, FF), D ** -0.5, 0.078125, ((0, 4), (1, 4), (2, 16)))
    w_down = scatter_about(streams_of[10], (EXPERTS, FF, D), FF ** -0.5, 0.078125, ((0, 4), (1, 16), (2, 4)))
    return dict(queries=queries, cache_keys=cache_keys, stored_values=stored_values, lengths=lengths, residual_in=residual_in, norm_gain=norm_gain, expert_ids=expert_ids, expert_scores=expert_scores, w_gate=w_gate, w_up=w_up, w_down=w_down)


epsilon = 1e-05

def attend_row(row_parts):
    query_slice, key_slice, value_slice, length_row = row_parts
    query_group = QUERY_HEADS // KEY_VALUE_HEADS
    query_float = query_slice.astype(jnp.float32).reshape(KEY_VALUE_HEADS, query_group, HEAD_SIZE)
    key_float = key_slice.astype(jnp.float32).reshape(CACHE_POSITIONS, KEY_VALUE_HEADS, HEAD_SIZE)
    value_float = value_slice.astype(jnp.float32).reshape(CACHE_POSITIONS, KEY_VALUE_HEADS, HEAD_SIZE)
    scores = jnp.einsum('hgd,lhd->hgl', query_float, key_float) * (1.0 / math.sqrt(HEAD_SIZE))
    position = jnp.arange(CACHE_POSITIONS, dtype=jnp.int32)
    visible = position < length_row
    scores = jnp.where(visible[None, None, :], scores, -1e+30)
    peak = lax.optimization_barrier(jnp.max(scores, axis=-1, keepdims=True))
    expd = jnp.exp(scores - peak)
    totals = lax.optimization_barrier(jnp.sum(expd, axis=-1, keepdims=True))
    weights_bf = (expd / totals).astype(jnp.bfloat16)
    attended = jnp.einsum('hgl,lhd->hgd', weights_bf.astype(jnp.float32), value_float)
    return attended.reshape(QUERY_HEADS * HEAD_SIZE).astype(jnp.bfloat16)

def reference(queries, cache_keys, stored_values, lengths, residual_in, norm_gain, expert_ids, expert_scores, w_gate, w_up, w_down):
    attended = lax.map(attend_row, (queries, cache_keys, stored_values, lengths))
    stream = (residual_in.astype(jnp.float32) + attended.astype(jnp.float32)).astype(jnp.bfloat16)
    stream_f = stream.astype(jnp.float32)
    row_mean = lax.optimization_barrier(jnp.mean(stream_f, axis=1, keepdims=True))
    row_var = lax.optimization_barrier(jnp.mean(jnp.square(stream_f - row_mean), axis=1, keepdims=True))
    normed = ((stream_f - row_mean) * lax.rsqrt(row_var + epsilon) * norm_gain.astype(jnp.float32)[None, :]).astype(jnp.bfloat16)
    shares = expert_scores / lax.optimization_barrier(jnp.sum(expert_scores, axis=1, keepdims=True))
    expert_iota = jnp.arange(EXPERTS, dtype=jnp.int32)
    route = lax.optimization_barrier(jnp.sum(jnp.where(expert_ids[:, :, None] == expert_iota[None, None, :], shares[:, :, None], 0.0), axis=1)).astype(jnp.bfloat16)

    def one_expert(total, index):
        gate_sum = jnp.dot(normed, w_gate[index], preferred_element_type=jnp.float32)
        up_sum = jnp.dot(normed, w_up[index], preferred_element_type=jnp.float32)
        weight_col = lax.dynamic_slice_in_dim(route, index, 1, 1).astype(jnp.float32)
        hidden = (jax.nn.silu(gate_sum) * up_sum * weight_col).astype(jnp.bfloat16)
        return (total + jnp.dot(hidden, w_down[index], preferred_element_type=jnp.float32), None)
    start_total = jnp.zeros((DECODE_ROWS, D), jnp.float32)
    mixed, _ = lax.scan(one_expert, start_total, jnp.arange(EXPERTS, dtype=jnp.int32))
    return (stream, mixed.astype(jnp.bfloat16))
```

```python
import math

import jax
import jax.numpy as jnp
from jax import lax
from jax.sharding import PartitionSpec as P

HEAD_SIZE = 128
EXPERTS = 8

epsilon = 1e-05
f32, bf16 = jnp.float32, jnp.bfloat16


def attend(queries, cache_keys, stored_values, lengths):
    row_count = queries.shape[0]
    span = cache_keys.shape[1]
    kv_heads = cache_keys.shape[2] // HEAD_SIZE
    query_group = queries.shape[1] // (kv_heads * HEAD_SIZE)
    query_blocks = queries.reshape(row_count, kv_heads, query_group, HEAD_SIZE)
    key_blocks = cache_keys.reshape(row_count, span, kv_heads, HEAD_SIZE)
    value_blocks = stored_values.reshape(row_count, span, kv_heads, HEAD_SIZE)
    scores = jnp.einsum(
        "rhgd,rlhd->rhgl", query_blocks, key_blocks, preferred_element_type=f32
    ) * (1.0 / math.sqrt(HEAD_SIZE))
    position = lax.broadcasted_iota(jnp.int32, (1, 1, 1, span), 3)
    visible = position < lengths[:, None, None, None]
    scores = jnp.where(visible, scores, -1e30)
    peak = jnp.max(scores, axis=-1, keepdims=True)
    expd = jnp.exp(scores - peak)
    totals = jnp.sum(expd, axis=-1, keepdims=True)
    weights_bf = (expd / totals).astype(bf16)
    attended = jnp.einsum(
        "rhgl,rlhd->rhgd", weights_bf, value_blocks, preferred_element_type=f32
    )
    return attended.reshape(row_count, kv_heads * query_group * HEAD_SIZE).astype(bf16)


def shift(x, axis, step):
    n = lax.axis_size(axis)
    return lax.ppermute(x, axis, [(i, (i + step) % n) for i in range(n)])


def swap_core(x):
    return lax.ppermute(x, "attn", [(i, i ^ 1) for i in range(lax.axis_size("attn"))])


def per_device(
    queries,
    cache_keys,
    stored_values,
    lengths,
    residual_in,
    norm_gain,
    expert_ids,
    expert_scores,
    w_gate,
    w_up,
    w_down,
):
    z_size, x_size, y_size = lax.axis_size("attn") // 2, lax.axis_size("egrp"), lax.axis_size("etp")
    y, x = lax.axis_index("etp"), lax.axis_index("egrp")
    attended = attend(queries, cache_keys, stored_values, lengths)
    stream = (residual_in.astype(f32) + attended.astype(f32)).astype(bf16)
    rows, width = stream.shape
    shares = expert_scores / jnp.sum(expert_scores, axis=1, keepdims=True)
    expert_iota = lax.broadcasted_iota(jnp.int32, (1, 1, EXPERTS), 2)
    route = jnp.sum(
        jnp.where(expert_ids[:, :, None] == expert_iota, shares[:, :, None], 0.0), axis=1
    ).astype(bf16)

    held = jnp.concatenate([stream, jnp.pad(route, ((0, 0), (0, 128 - EXPERTS)))], axis=1)
    held = jnp.concatenate([held] + [shift(held, "attn", -2 * k) for k in range(1, z_size)], axis=0)
    held = jnp.concatenate([held] + [shift(held, "egrp", -k) for k in range(1, x_size)], axis=0)
    held = jnp.concatenate([held, swap_core(held)], axis=0)
    raw, routes = held[:, :width].astype(f32), held[:, width : width + EXPERTS]
    total = raw.shape[0]

    part_mean = jnp.mean(raw, axis=1)
    centred = raw - part_mean[:, None]
    part_dev = jnp.sum(jnp.square(centred), axis=1)
    stats = jnp.stack([part_mean, part_dev])
    all_stats = [stats] + [shift(stats, "etp", k) for k in range(1, y_size)]
    row_mean = sum(s[0] for s in all_stats) / y_size
    row_dev = sum(s[1] + width * jnp.square(s[0] - row_mean) for s in all_stats)
    row_scale = lax.rsqrt(row_dev / (width * y_size) + epsilon)

    gain = lax.dynamic_slice_in_dim(norm_gain, y * width, width, 0)
    scaled = (centred * gain.astype(f32)[None, :]).astype(bf16)
    gains = jnp.broadcast_to(gain[None, :], (8, width))

    def project(weight):
        part = jnp.einsum("edf,rd->efr", weight, scaled, preferred_element_type=f32)
        sums = jnp.einsum("edf,rd->efr", weight, gains, preferred_element_type=f32)[:, :, :1]
        return (part + sums * (part_mean - row_mean)[None, None, :]) * row_scale[None, None, :]

    both = jnp.stack([project(w_gate), project(w_up)])

    block = total // y_size

    def block_of(array, index):
        return lax.dynamic_slice_in_dim(array, lax.rem(index, y_size) * block, block, array.ndim - 1)

    mine = block_of(both, y)
    for k in range(1, y_size):
        mine = mine + shift(block_of(both, y + k).astype(bf16), "etp", k).astype(f32)
    experts_here = w_gate.shape[0]
    route_rows = lax.dynamic_slice(
        routes, (y * block, x * experts_here), (block, experts_here)
    ).astype(f32)
    hidden = (jax.nn.silu(mine[0]) * mine[1] * route_rows.T[:, None, :]).astype(bf16)
    turned = [hidden] + [shift(hidden, "etp", -k) for k in range(1, y_size)]
    whole = jnp.concatenate(turned + turned[:-1], axis=2)
    whole = lax.dynamic_slice_in_dim(whole, lax.rem(y_size - y, y_size) * block, total, 2)

    out = jnp.einsum("efr,efd->rd", whole, w_down, preferred_element_type=f32)
    half = total // 2
    out = out[:half] + swap_core(out[half:].astype(bf16)).astype(f32)
    for axis, size, stride in (("egrp", x_size, 1), ("attn", z_size, 2)):
        part = out.shape[0] // size
        summed = out[:part]
        for k in range(1, size):
            sent = out[k * part : (k + 1) * part].astype(bf16)
            summed = summed + shift(sent, axis, stride * k).astype(f32)
        out = summed
    return (stream, out.astype(bf16))


def solution(mesh):
    placed = (
        P(("attn", "egrp"), "etp"),
        P(("attn", "egrp"), None, "etp"),
        P(("attn", "egrp"), None, "etp"),
        P(("attn", "egrp")),
        P(("attn", "egrp"), "etp"),
        P(),
        P(("attn", "egrp"), None),
        P(("attn", "egrp"), None),
        P("egrp", "etp", "attn"),
        P("egrp", "etp", "attn"),
        P("egrp", "attn", "etp"),
    )
    return jax.shard_map(
        per_device,
        mesh=mesh,
        in_specs=placed,
        out_specs=(P(("attn", "egrp"), "etp"), P(("attn", "egrp"), "etp")),
        check_vma=False,
    )
```

```python
import math

import jax
import jax.numpy as jnp
from jax import lax
from jax.experimental import pallas as pl
from jax.experimental.pallas import tpu as pltpu
from jax.sharding import PartitionSpec as P

HEAD_SIZE = 128
EXPERTS = 8

epsilon = 1e-05
f32, bf16 = jnp.float32, jnp.bfloat16


def attend(queries, cache_keys, stored_values, lengths):
    row_count = queries.shape[0]
    span = cache_keys.shape[1]
    kv_heads = cache_keys.shape[2] // HEAD_SIZE
    query_group = queries.shape[1] // (kv_heads * HEAD_SIZE)
    query_blocks = queries.reshape(row_count, kv_heads, query_group, HEAD_SIZE)
    key_blocks = cache_keys.reshape(row_count, span, kv_heads, HEAD_SIZE)
    value_blocks = stored_values.reshape(row_count, span, kv_heads, HEAD_SIZE)
    scores = jnp.einsum(
        "rhgd,rlhd->rhgl", query_blocks, key_blocks, preferred_element_type=f32
    ) * (1.0 / math.sqrt(HEAD_SIZE))
    position = lax.broadcasted_iota(jnp.int32, (1, 1, 1, span), 3)
    visible = position < lengths[:, None, None, None]
    scores = jnp.where(visible, scores, -1e30)
    peak = jnp.max(scores, axis=-1, keepdims=True)
    expd = jnp.exp(scores - peak)
    totals = jnp.sum(expd, axis=-1, keepdims=True)
    weights_bf = (expd / totals).astype(bf16)
    attended = jnp.einsum(
        "rhgl,rlhd->rhgd", weights_bf, value_blocks, preferred_element_type=f32
    )
    return attended.reshape(row_count, kv_heads * query_group * HEAD_SIZE).astype(bf16)


def send(x, axes, target):
    sizes = [lax.axis_size(axis) for axis in axes]
    pairs = []
    for index in range(math.prod(sizes)):
        place, rest = [], index
        for size in reversed(sizes):
            place.insert(0, rest % size)
            rest //= size
        other = 0
        for coordinate, size in zip(target(*place), sizes):
            other = other * size + coordinate % size
        pairs.append((index, other))
    return lax.ppermute(x, axes, pairs)


def swap_core(x):
    return send(x, ("attn",), lambda a: (a ^ 1,))


def along_z(x, step, back=False):
    sign = 1 if back else -1
    return send(x, ("attn",), lambda a: (a + sign * 2 * (step if a % 2 == 0 else -step),))


def along_x(x, step):
    return send(x, ("attn", "egrp"), lambda a, i: (a, i ^ (2 if step == 2 else 1 if a % 2 == step else 3)))


def to_y(x, step):
    return send(x, ("etp",), lambda i: (i + step,))


VMEM, SMEM, ANY = pltpu.VMEM, pltpu.SMEM, pl.ANY
NT = (((1,), (1,)), ((), ()))
CAPACITY_OF_512 = 384


def chosen(ranks, slots):
    slot = lax.broadcasted_iota(jnp.int32, (slots, ranks.shape[1]), 0)
    return (slot.astype(f32) == ranks).astype(bf16)


def pack_kernel(place, own, other, gate_own, gate_other, up_own, up_other, *outs):
    *outs, share, ranks = outs
    y, first = place[0], place[1]
    experts, fan, n = gate_own.shape
    units, slots = outs[0].shape[1], outs[0].shape[2]
    rows, extra = 2 * n, own.shape[1]
    route = jnp.concatenate([own[...], other[...]], axis=0)
    named = (route.astype(f32) > 0.0).astype(bf16)
    before = lax.broadcasted_iota(jnp.int32, (rows, rows), 1) <= lax.broadcasted_iota(
        jnp.int32, (rows, rows), 0
    )
    counts = jnp.dot(before.astype(bf16), named, preferred_element_type=f32)
    placed = jnp.where(named > 0, counts - 1.0, -1.0)
    column = lax.broadcasted_iota(jnp.int32, (rows, extra), 1)
    slot = lax.broadcasted_iota(jnp.int32, (rows, slots), 1).astype(f32)
    ranks[...] = jnp.transpose(placed)
    for e in range(experts):
        here = column == first + e
        rank = jnp.sum(jnp.where(here, placed, 0.0), axis=1, keepdims=True)
        onehot = (slot == rank).astype(bf16)

        @pl.when(y // (len(outs) // experts) == e)
        def _():
            values = jnp.sum(jnp.where(here, route.astype(f32), 0.0), axis=1, keepdims=True)
            values = jnp.sum(onehot.astype(f32) * values, axis=0, keepdims=True)
            share[...] = jnp.broadcast_to(values, share.shape)

        for g, (part_own, part_other) in enumerate(((gate_own, gate_other), (up_own, up_other))):
            packed = jnp.dot(part_own[e], onehot[:n], preferred_element_type=f32)
            packed = packed + jnp.dot(part_other[e], onehot[n:], preferred_element_type=f32)
            for h in range(fan // units):
                part = packed[h * units : (h + 1) * units].astype(bf16)
                step = lax.rem(e * (fan // units) + h + len(outs) - y, len(outs))
                for k, out in enumerate(outs):

                    @pl.when(step == k)
                    def _(out=out, g=g, part=part):
                        out[g] = part


def pack(place, own, other, sums):
    experts, fan, n = sums[0].shape
    rows, extra = 2 * n, own.shape[1]
    parts, slots = 4, rows * CAPACITY_OF_512 // 512
    whole = pl.BlockSpec(memory_space=VMEM)
    return pl.pallas_call(
        pack_kernel,
        out_shape=[jax.ShapeDtypeStruct((2, experts * fan // parts, slots), bf16)] * parts
        + [jax.ShapeDtypeStruct((8, slots), f32), jax.ShapeDtypeStruct((extra, rows), f32)],
        in_specs=[pl.BlockSpec(memory_space=SMEM)] + [whole] * 6,
        out_specs=[whole] * (parts + 2),
        compiler_params=pltpu.CompilerParams(vmem_limit_bytes=16 << 20),
        cost_estimate=pl.CostEstimate(flops=1 << 29, bytes_accessed=2 << 20, transcendentals=0),
    )(place, own, other, *sums)


def split_kernel(*refs):
    *pieces, rows, features, routes = refs
    width, at = features.shape[1], 0
    for piece in pieces:
        count = piece.shape[0]
        if rows is not None:
            rows[at : at + count] = piece[...]
        features[at : at + count] = piece[:, :width]
        routes[at : at + count] = piece[:, width:]
        at += count


def split(pieces, width, joined):
    count, columns = sum(p.shape[0] for p in pieces), pieces[0].shape[1]
    whole = pl.BlockSpec(memory_space=VMEM)
    widths = [columns] * joined + [width, columns - width]

    def kernel(*refs):
        outs = refs[len(pieces) :]
        split_kernel(*refs[: len(pieces)], outs[0] if joined else None, *outs[-2:])

    return pl.pallas_call(
        kernel,
        out_shape=[jax.ShapeDtypeStruct((count, w), pieces[0].dtype) for w in widths],
        in_specs=[whole] * len(pieces),
        out_specs=[whole] * len(widths),
        compiler_params=pltpu.CompilerParams(vmem_limit_bytes=8 << 20),
        cost_estimate=pl.CostEstimate(flops=1, bytes_accessed=1 << 20, transcendentals=0),
    )(*pieces)


def scatter_kernel(place, hidden0, hidden1, hidden2, hidden3, ranks, out):
    parts, slots = out.shape[0], hidden0.shape[1]
    for k, hidden in enumerate((hidden0, hidden1, hidden2, hidden3)):
        at = lax.rem(place[0] + k, parts)
        onehot = chosen(ranks[pl.ds(place[1] + at // 2, 1), :], slots)
        out[at] = jnp.dot(hidden[...], onehot, preferred_element_type=f32).astype(bf16)


def scatter(place, hidden, ranks):
    whole = pl.BlockSpec(memory_space=VMEM)
    return pl.pallas_call(
        scatter_kernel,
        out_shape=jax.ShapeDtypeStruct((4, hidden[0].shape[0], ranks.shape[1]), bf16),
        in_specs=[pl.BlockSpec(memory_space=SMEM)] + [whole] * 5,
        out_specs=whole,
        compiler_params=pltpu.CompilerParams(vmem_limit_bytes=16 << 20),
        cost_estimate=pl.CostEstimate(flops=1 << 28, bytes_accessed=1 << 20, transcendentals=0),
    )(place, *hidden, ranks)


def per_device(
    queries,
    cache_keys,
    stored_values,
    lengths,
    residual_in,
    norm_gain,
    expert_ids,
    expert_scores,
    w_gate,
    w_up,
    w_down,
):
    y, x = lax.axis_index("etp"), lax.axis_index("egrp")
    y_size = lax.axis_size("etp")
    attended = attend(queries, cache_keys, stored_values, lengths)
    stream = (residual_in.astype(f32) + attended.astype(f32)).astype(bf16)
    rows, width = stream.shape
    shares = expert_scores / jnp.sum(expert_scores, axis=1, keepdims=True)
    expert_iota = lax.broadcasted_iota(jnp.int32, (1, 1, EXPERTS), 2)
    route = jnp.sum(
        jnp.where(expert_ids[:, :, None] == expert_iota, shares[:, :, None], 0.0), axis=1
    ).astype(bf16)

    raw = stream.astype(f32)
    part_mean = jnp.mean(raw, axis=1, keepdims=True)
    part_dev = jnp.sum(jnp.square(raw - part_mean), axis=1, keepdims=True)
    stats = jnp.concatenate([part_mean, part_dev], axis=1)
    stats = [stats] + [to_y(stats, k) for k in range(1, y_size)]
    mean = sum(s[:, :1] for s in stats) / y_size
    dev = sum(s[:, 1:] + width * jnp.square(s[:, :1] - mean) for s in stats)
    gain = lax.dynamic_slice_in_dim(norm_gain, y * width, width, 0).astype(f32)
    normed = (raw - mean) * lax.rsqrt(dev / (width * y_size) + epsilon) * gain[None, :]
    held = jnp.concatenate(
        [normed.astype(bf16), jnp.pad(route, ((0, 0), (0, 128 - EXPERTS)))], axis=1
    )

    place = jnp.stack([y, x * w_gate.shape[0]]).astype(jnp.int32)
    down = w_down.reshape(-1, width)

    def project(weight, tokens):
        return jnp.einsum("edf,rd->efr", weight, tokens, preferred_element_type=f32).astype(bf16)

    across = along_z(held, 4)
    chip = jnp.concatenate([held, swap_core(held)], axis=0)
    held = jnp.concatenate([held, across] + [along_z(chip, k) for k in (1, 2, 3)], axis=0)
    own, own_rows, own_routes = split([held] + [along_x(held, k) for k in range(3)], width, True)
    other_rows, other_routes = split([swap_core(own)], width, False)
    sums = [project(w, t) for w in (w_gate, w_up) for t in (own_rows, other_rows)]
    *parts, share, ranks = pack(place, own_routes, other_routes, sums)
    sums = parts[0].astype(f32) + sum(
        to_y(part, k).astype(f32) for k, part in enumerate(parts) if k > 0
    )
    hidden = (jax.nn.silu(sums[0]) * sums[1] * share[:1]).astype(bf16)
    hidden = scatter(place, [hidden] + [to_y(hidden, -k) for k in range(1, y_size)], ranks)
    hidden = hidden.reshape(down.shape[0], -1)
    n = own.shape[0]

    def back_down(at):
        return jnp.einsum("fr,fd->rd", hidden[:, at : at + n], down, preferred_element_type=f32)

    other = swap_core(back_down(n).astype(bf16))
    total = back_down(0) + other.astype(f32)
    n = n // 4
    total = total[:n] + sum(
        along_x(total[(k + 1) * n : (k + 2) * n].astype(bf16), k).astype(f32) for k in range(3)
    )
    mine, across, n = total[:rows], total[rows : 2 * rows].astype(bf16), 2 * rows
    chip = sum(
        along_z(total[k * n : (k + 1) * n].astype(bf16), k, True).astype(f32) for k in (1, 2, 3)
    )
    mine = mine + along_z(across, 4, True).astype(f32) + chip[:rows]
    mine = mine + swap_core(chip[rows:].astype(bf16)).astype(f32)
    return (stream, mine.astype(bf16))


def solution(mesh):
    placed = (
        P(("attn", "egrp"), "etp"),
        P(("attn", "egrp"), None, "etp"),
        P(("attn", "egrp"), None, "etp"),
        P(("attn", "egrp")),
        P(("attn", "egrp"), "etp"),
        P(),
        P(("attn", "egrp"), None),
        P(("attn", "egrp"), None),
        P("egrp", "etp", "attn"),
        P("egrp", "etp", "attn"),
        P("egrp", "attn", "etp"),
    )
    return jax.shard_map(
        per_device,
        mesh=mesh,
        in_specs=placed,
        out_specs=(P(("attn", "egrp"), "etp"), P(("attn", "egrp"), "etp")),
        check_vma=False,
    )
```

```python
import math

import jax
import jax.numpy as jnp
from jax import lax
from jax.experimental import pallas as pl
from jax.experimental.pallas import tpu as pltpu
from jax.sharding import PartitionSpec as P

HEAD_SIZE = 128
EXPERTS = 8

epsilon = 1e-05
PART_WIDTH = 1536
f32, bf16 = jnp.float32, jnp.bfloat16


def attend(queries, cache_keys, stored_values, lengths):
    row_count = queries.shape[0]
    span = cache_keys.shape[1]
    kv_heads = cache_keys.shape[2] // HEAD_SIZE
    query_group = queries.shape[1] // (kv_heads * HEAD_SIZE)
    query_blocks = queries.reshape(row_count, kv_heads, query_group, HEAD_SIZE)
    key_blocks = cache_keys.reshape(row_count, span, kv_heads, HEAD_SIZE)
    value_blocks = stored_values.reshape(row_count, span, kv_heads, HEAD_SIZE)
    scores = jnp.einsum(
        "rhgd,rlhd->rhgl", query_blocks, key_blocks, preferred_element_type=f32
    ) * (1.0 / math.sqrt(HEAD_SIZE))
    position = lax.broadcasted_iota(jnp.int32, (1, 1, 1, span), 3)
    visible = position < lengths[:, None, None, None]
    scores = jnp.where(visible, scores, -1e30)
    peak = jnp.max(scores, axis=-1, keepdims=True)
    expd = jnp.exp(scores - peak)
    totals = jnp.sum(expd, axis=-1, keepdims=True)
    weights_bf = (expd / totals).astype(bf16)
    attended = jnp.einsum(
        "rhgl,rlhd->rhgd", weights_bf, value_blocks, preferred_element_type=f32
    )
    return attended.reshape(row_count, kv_heads * query_group * HEAD_SIZE)


def send(x, axes, target):
    sizes = [lax.axis_size(axis) for axis in axes]
    pairs = []
    for index in range(math.prod(sizes)):
        place, rest = [], index
        for size in reversed(sizes):
            place.insert(0, rest % size)
            rest //= size
        other = 0
        for coordinate, size in zip(target(*place), sizes):
            other = other * size + coordinate % size
        pairs.append((index, other))
    return lax.ppermute(x, axes, pairs)


def swap_core(x):
    return send(x, ("attn",), lambda a: (a ^ 1,))


def along_z(x, step, back=False):
    sign = 1 if back else -1
    return send(x, ("attn",), lambda a: (a + sign * 2 * (step if a % 2 == 0 else -step),))


def along_x(x, step):
    return send(x, ("attn", "egrp"), lambda a, i: (a, i ^ (2 if step == 2 else 1 if a % 2 == step else 3)))


def to_y(x, step):
    return send(x, ("etp",), lambda i: (i + step,))


VMEM, SMEM, ANY = pltpu.VMEM, pltpu.SMEM, pl.ANY
NT = (((1,), (1,)), ((), ()))
CAPACITY_OF_512 = 384


def finish_kernel(place, attended, residual, gain, ids, scores, stream, held):
    rows, width = attended.shape
    column = lax.broadcasted_iota(jnp.int32, (rows, held.shape[1] - width), 1)
    share = scores[...] / jnp.sum(scores[...], axis=0, keepdims=True)
    share, named = jnp.transpose(share), jnp.transpose(ids[...].astype(f32))
    notes = jnp.zeros(column.shape, f32)
    for k in range(named.shape[1]):
        here = column.astype(f32) == named[:, k : k + 1]
        notes = notes + jnp.where(here, share[:, k : k + 1], 0.0)
    summed = residual[...].astype(f32) + attended[...].astype(bf16).astype(f32)
    stream[...] = summed.astype(bf16)
    raw = summed.astype(bf16).astype(f32)
    mean = jnp.sum(raw, axis=1, keepdims=True) / width
    centred = raw - mean
    dev = jnp.sum(jnp.square(centred), axis=1, keepdims=True)
    at = EXPERTS
    for rest in (mean, dev):
        for _ in range(3):
            term = rest.astype(bf16).astype(f32)
            notes = jnp.where(column == at, term, notes)
            rest, at = rest - term, at + 1
    own = gain[pl.ds(pl.multiple_of(place[0] * width, width), width)]
    held[:, :width] = (centred * own.astype(f32).reshape(1, width)).astype(bf16)
    held[:, width:] = notes.astype(bf16)


def finish(place, attended, residual, gain, ids, scores):
    whole = pl.BlockSpec(memory_space=VMEM)
    rows, width = attended.shape
    return pl.pallas_call(
        finish_kernel,
        out_shape=[
            jax.ShapeDtypeStruct((rows, width), bf16),
            jax.ShapeDtypeStruct((rows, width + 128), bf16),
        ],
        in_specs=[pl.BlockSpec(memory_space=SMEM)] + [whole] * 5,
        out_specs=[whole] * 2,
        compiler_params=pltpu.CompilerParams(vmem_limit_bytes=4 << 20),
        cost_estimate=pl.CostEstimate(flops=1 << 16, bytes_accessed=1 << 16, transcendentals=0),
    )(place, attended, residual, gain, ids, scores)


def chosen(ranks, slots):
    slot = lax.broadcasted_iota(jnp.int32, (slots, ranks.shape[1]), 0)
    return (slot.astype(f32) == ranks).astype(bf16)


def pack_kernel(place, own, other, gate_own, gate_other, up_own, up_other, *outs):
    *outs, share, ranks = outs
    y, first = place[0], place[1]
    experts, fan, n = gate_own.shape
    slots, units = outs[0].shape[2], experts * fan // len(outs)
    rows, extra = 2 * n, own.shape[1]
    notes = jnp.concatenate([own[...], other[...]], axis=0).astype(f32)
    named = notes > 0.0
    before = lax.broadcasted_iota(jnp.int32, (rows, rows), 1) <= lax.broadcasted_iota(
        jnp.int32, (rows, rows), 0
    )
    counts = jnp.dot(
        before.astype(bf16), jnp.where(named, 1.0, 0.0).astype(bf16), preferred_element_type=f32
    )
    placed = jnp.where(named, counts - 1.0, -1.0)
    column = lax.broadcasted_iota(jnp.int32, (rows, extra), 1)
    slot = lax.broadcasted_iota(jnp.int32, (rows, slots), 1).astype(f32)
    ranks[...] = jnp.transpose(placed)
    turned = jnp.transpose(notes)[: 2 * EXPERTS].astype(bf16)
    line = lax.broadcasted_iota(jnp.int32, (2 * EXPERTS, slots), 0)
    for e in range(experts):
        rank = jnp.sum(jnp.where(column == first + e, placed, 0.0), axis=1, keepdims=True)
        onehot = (slot == rank).astype(bf16)
        listed = jnp.dot(turned, onehot, preferred_element_type=f32)
        stats = listed[EXPERTS:]

        @pl.when(y // (len(outs) // experts) == e)
        def _():
            values = jnp.sum(jnp.where(line == first + e, listed, 0.0), axis=0, keepdims=True)
            share[...] = jnp.broadcast_to(values, share.shape)

        for g, (part_own, part_other) in enumerate(((gate_own, gate_other), (up_own, up_other))):
            packed = jnp.dot(part_own[e], onehot[:n], preferred_element_type=f32)
            packed = packed + jnp.dot(part_other[e], onehot[n:], preferred_element_type=f32)
            for h in range(fan // units):
                part = jnp.concatenate([packed[h * units : (h + 1) * units], stats], axis=0)
                part = part.astype(bf16)
                step = lax.rem(e * (fan // units) + h + len(outs) - y, len(outs))
                for k, out in enumerate(outs):

                    @pl.when(step == k)
                    def _(out=out, g=g, part=part):
                        out[g] = part


def pack(place, own, other, sums):
    experts, fan, n = sums[0].shape
    rows, extra = 2 * n, own.shape[1]
    parts, slots = 4, rows * CAPACITY_OF_512 // 512
    whole = pl.BlockSpec(memory_space=VMEM)
    return pl.pallas_call(
        pack_kernel,
        out_shape=[jax.ShapeDtypeStruct((2, experts * fan // parts + EXPERTS, slots), bf16)] * parts
        + [jax.ShapeDtypeStruct((8, slots), f32), jax.ShapeDtypeStruct((extra, rows), f32)],
        in_specs=[pl.BlockSpec(memory_space=SMEM)] + [whole] * 6,
        out_specs=[whole] * (parts + 2),
        compiler_params=pltpu.CompilerParams(vmem_limit_bytes=16 << 20),
        cost_estimate=pl.CostEstimate(flops=1 << 29, bytes_accessed=2 << 20, transcendentals=0),
    )(place, own, other, *sums)


def split_kernel(*refs):
    *pieces, rows, features, routes = refs
    width, at = features.shape[1], 0
    for piece in pieces:
        count = piece.shape[0]
        if rows is not None:
            rows[at : at + count] = piece[...]
        features[at : at + count] = piece[:, :width]
        routes[at : at + count] = piece[:, width:]
        at += count


def split(pieces, width, joined):
    count, columns = sum(p.shape[0] for p in pieces), pieces[0].shape[1]
    whole = pl.BlockSpec(memory_space=VMEM)
    widths = [columns] * joined + [width, columns - width]

    def kernel(*refs):
        outs = refs[len(pieces) :]
        split_kernel(*refs[: len(pieces)], outs[0] if joined else None, *outs[-2:])

    return pl.pallas_call(
        kernel,
        out_shape=[jax.ShapeDtypeStruct((count, w), pieces[0].dtype) for w in widths],
        in_specs=[whole] * len(pieces),
        out_specs=[whole] * len(widths),
        compiler_params=pltpu.CompilerParams(vmem_limit_bytes=8 << 20),
        cost_estimate=pl.CostEstimate(flops=1, bytes_accessed=1 << 20, transcendentals=0),
    )(*pieces)


def activate_kernel(part0, part1, part2, part3, gains, share, hidden):
    parts = [[p[g].astype(f32) for g in range(2)] for p in (part0, part1, part2, part3)]
    units, slots = hidden.shape
    count = len(parts)
    means, devs = [], []
    for part in parts:
        stats = part[0][units:]
        means.append(stats[0:1] + stats[1:2] + stats[2:3])
        devs.append(stats[3:4] + stats[4:5] + stats[5:6])
    mean = sum(means) / count
    var = sum(devs) / (count * PART_WIDTH)
    var = var + sum(jnp.square(m - mean) for m in means) / count
    scale = lax.rsqrt(var + epsilon)
    columns = jnp.transpose(gains[...])

    def total(g):
        result = sum(part[g][:units] for part in parts)
        for k in range(count):
            result = result + columns[:, 2 * k + g : 2 * k + g + 1] * (means[k] - mean)
        return result * scale

    gate = total(0)
    hidden[...] = (gate * jax.nn.sigmoid(gate) * total(1) * share[0:1]).astype(bf16)


def activate(parts, gains, share):
    whole = pl.BlockSpec(memory_space=VMEM)
    units, slots = parts[0].shape[1] - EXPERTS, parts[0].shape[2]
    return pl.pallas_call(
        activate_kernel,
        out_shape=jax.ShapeDtypeStruct((units, slots), bf16),
        in_specs=[whole] * 6,
        out_specs=whole,
        compiler_params=pltpu.CompilerParams(vmem_limit_bytes=8 << 20),
        cost_estimate=pl.CostEstimate(flops=1, bytes_accessed=1 << 20, transcendentals=1),
    )(*parts, gains, share)


def scatter_kernel(place, hidden0, hidden1, hidden2, hidden3, ranks, out):
    parts, slots = out.shape[0], hidden0.shape[1]
    for k, hidden in enumerate((hidden0, hidden1, hidden2, hidden3)):
        at = lax.rem(place[0] + k, parts)
        onehot = chosen(ranks[pl.ds(place[1] + at // 2, 1), :], slots)
        out[at] = jnp.dot(hidden[...], onehot, preferred_element_type=f32).astype(bf16)


def scatter(place, hidden, ranks):
    whole = pl.BlockSpec(memory_space=VMEM)
    return pl.pallas_call(
        scatter_kernel,
        out_shape=jax.ShapeDtypeStruct((4, hidden[0].shape[0], ranks.shape[1]), bf16),
        in_specs=[pl.BlockSpec(memory_space=SMEM)] + [whole] * 5,
        out_specs=whole,
        compiler_params=pltpu.CompilerParams(vmem_limit_bytes=16 << 20),
        cost_estimate=pl.CostEstimate(flops=1 << 28, bytes_accessed=1 << 20, transcendentals=0),
    )(place, *hidden, ranks)


def per_device(
    queries,
    cache_keys,
    stored_values,
    lengths,
    residual_in,
    norm_gain,
    expert_ids,
    expert_scores,
    w_gate,
    w_up,
    w_down,
):
    y, x = lax.axis_index("etp"), lax.axis_index("egrp")
    y_size = lax.axis_size("etp")
    attended = attend(queries, cache_keys, stored_values, lengths)
    place = jnp.stack([y, x * w_gate.shape[0]]).astype(jnp.int32)
    stream, held = finish(place, attended, residual_in, norm_gain, expert_ids.T, expert_scores.T)
    rows, width = stream.shape
    gain = lax.dynamic_slice_in_dim(norm_gain, y * width, width, 0).astype(f32)

    down = w_down.reshape(-1, width)

    def project(weight, tokens):
        return jnp.einsum("edf,rd->efr", weight, tokens, preferred_element_type=f32).astype(bf16)

    across = along_z(held, 4)
    chip = jnp.concatenate([held, swap_core(held)], axis=0)
    held = jnp.concatenate([held, across] + [along_z(chip, k) for k in (1, 2, 3)], axis=0)
    gain, held = lax.optimization_barrier((gain, held))
    gains = jnp.stack(
        [jnp.einsum("edf,d->ef", w.astype(f32), gain).reshape(y_size, -1) for w in (w_gate, w_up)]
    )

    def gain_block(k):
        return lax.dynamic_index_in_dim(gains, lax.rem(y + k, y_size), 1, False)

    gains = [gain_block(0)] + [to_y(gain_block(k), k) for k in range(1, y_size)]
    pieces = [along_x(held, k) for k in range(3)]
    pieces, gains = lax.optimization_barrier((pieces, jnp.concatenate(gains, axis=0)))
    own, own_rows, own_notes = split([held] + pieces, width, True)
    other_rows, other_notes = split([swap_core(own)], width, False)
    sums = [project(w, t) for w in (w_gate, w_up) for t in (own_rows, other_rows)]
    *parts, share, ranks = pack(place, own_notes, other_notes, sums)
    parts = [parts[0]] + [to_y(part, k) for k, part in enumerate(parts) if k > 0]
    hidden = activate(parts, gains, share)
    hidden = scatter(place, [hidden] + [to_y(hidden, -k) for k in range(1, y_size)], ranks)
    hidden = hidden.reshape(down.shape[0], -1)
    n = own.shape[0]

    def back_down(at):
        return jnp.einsum("fr,fd->rd", hidden[:, at : at + n], down, preferred_element_type=f32)

    other = swap_core(back_down(n).astype(bf16))
    total = back_down(0) + other.astype(f32)
    n = n // 4
    total = total[:n] + sum(
        along_x(total[(k + 1) * n : (k + 2) * n].astype(bf16), k).astype(f32) for k in range(3)
    )
    mine, across, n = total[:rows], total[rows : 2 * rows].astype(bf16), 2 * rows
    chip = sum(
        along_z(total[k * n : (k + 1) * n].astype(bf16), k, True).astype(f32) for k in (1, 2, 3)
    )
    mine = mine + along_z(across, 4, True).astype(f32) + chip[:rows]
    mine = mine + swap_core(chip[rows:].astype(bf16)).astype(f32)
    return (stream, mine.astype(bf16))


def solution(mesh):
    placed = (
        P(("attn", "egrp"), "etp"),
        P(("attn", "egrp"), None, "etp"),
        P(("attn", "egrp"), None, "etp"),
        P(("attn", "egrp")),
        P(("attn", "egrp"), "etp"),
        P(),
        P(("attn", "egrp"), None),
        P(("attn", "egrp"), None),
        P("egrp", "etp", "attn"),
        P("egrp", "etp", "attn"),
        P("egrp", "attn", "etp"),
    )
    return jax.shard_map(
        per_device,
        mesh=mesh,
        in_specs=placed,
        out_specs=(P(("attn", "egrp"), "etp"), P(("attn", "egrp"), "etp")),
        check_vma=False,
    )
```

```python
import math

import jax
import jax.numpy as jnp
from jax import lax
from jax.experimental import pallas as pl
from jax.experimental.pallas import tpu as pltpu
from jax.sharding import PartitionSpec as P

HEAD_SIZE = 128
EXPERTS = 8

epsilon = 1e-05
PART_WIDTH = 1536
f32, bf16 = jnp.float32, jnp.bfloat16


def attend(queries, cache_keys, stored_values, lengths):
    row_count = queries.shape[0]
    span = cache_keys.shape[1]
    kv_heads = cache_keys.shape[2] // HEAD_SIZE
    query_group = queries.shape[1] // (kv_heads * HEAD_SIZE)
    query_blocks = queries.reshape(row_count, kv_heads, query_group, HEAD_SIZE)
    key_blocks = cache_keys.reshape(row_count, span, kv_heads, HEAD_SIZE)
    value_blocks = stored_values.reshape(row_count, span, kv_heads, HEAD_SIZE)
    scores = jnp.einsum(
        "rhgd,rlhd->rhgl", query_blocks, key_blocks, preferred_element_type=f32
    ) * (1.0 / math.sqrt(HEAD_SIZE))
    position = lax.broadcasted_iota(jnp.int32, scores.shape, 3)
    visible = position < jnp.broadcast_to(lengths[:, None, None, None], scores.shape)
    scores = jnp.where(visible, scores, -1e30)
    peak = jnp.max(scores, axis=-1, keepdims=True)
    expd = jnp.exp(scores - peak)
    totals = jnp.sum(expd, axis=-1, keepdims=True)
    weights_bf = (expd / totals).astype(bf16)
    attended = jnp.einsum(
        "rhgl,rlhd->rhgd", weights_bf, value_blocks, preferred_element_type=f32
    )
    return attended.reshape(row_count, kv_heads * query_group * HEAD_SIZE)


def send(x, axes, target):
    sizes = [lax.axis_size(axis) for axis in axes]
    pairs = []
    for index in range(math.prod(sizes)):
        place, rest = [], index
        for size in reversed(sizes):
            place.insert(0, rest % size)
            rest //= size
        other = 0
        for coordinate, size in zip(target(*place), sizes):
            other = other * size + coordinate % size
        pairs.append((index, other))
    return lax.ppermute(x, axes, pairs)


def swap_core(x):
    return send(x, ("attn",), lambda a: (a ^ 1,))


def along_z(x, step, back=False):
    sign = 1 if back else -1
    return send(x, ("attn",), lambda a: (a + sign * 2 * (step if a % 2 == 0 else -step),))


def along_x(x, step):
    return send(x, ("attn", "egrp"), lambda a, i: (a, i ^ (2 if step == 2 else 1 if a % 2 == step else 3)))


def to_y(x, step):
    return send(x, ("etp",), lambda i: (i + step,))


VMEM, SMEM, ANY = pltpu.VMEM, pltpu.SMEM, pl.ANY
NT = (((1,), (1,)), ((), ()))
CAPACITY_OF_512 = 384


def finish_kernel(place, attended, residual, gain, ids, scores, stream, held):
    rows, width = attended.shape
    column = lax.broadcasted_iota(jnp.int32, (rows, held.shape[1] - width), 1)
    share = scores[...] / jnp.sum(scores[...], axis=0, keepdims=True)
    share, named = jnp.transpose(share), jnp.transpose(ids[...].astype(f32))
    notes = jnp.zeros(column.shape, f32)
    for k in range(named.shape[1]):
        here = column.astype(f32) == named[:, k : k + 1]
        notes = notes + jnp.where(here, share[:, k : k + 1], 0.0)
    summed = residual[...].astype(f32) + attended[...].astype(bf16).astype(f32)
    stream[...] = summed.astype(bf16)
    raw = summed.astype(bf16).astype(f32)
    mean = jnp.sum(raw, axis=1, keepdims=True) / width
    centred = raw - mean
    dev = jnp.sum(jnp.square(centred), axis=1, keepdims=True)
    at = EXPERTS
    for rest in (mean, dev):
        for _ in range(3):
            term = rest.astype(bf16).astype(f32)
            notes = jnp.where(column == at, term, notes)
            rest, at = rest - term, at + 1
    own = gain[pl.ds(pl.multiple_of(place[0] * width, width), width)]
    held[:, :width] = (centred * own.astype(f32).reshape(1, width)).astype(bf16)
    held[:, width:] = notes.astype(bf16)


def finish(place, attended, residual, gain, ids, scores):
    whole = pl.BlockSpec(memory_space=VMEM)
    rows, width = attended.shape
    return pl.pallas_call(
        finish_kernel,
        out_shape=[
            jax.ShapeDtypeStruct((rows, width), bf16),
            jax.ShapeDtypeStruct((rows, width + 128), bf16),
        ],
        in_specs=[pl.BlockSpec(memory_space=SMEM)] + [whole] * 5,
        out_specs=[whole] * 2,
        compiler_params=pltpu.CompilerParams(vmem_limit_bytes=4 << 20),
        cost_estimate=pl.CostEstimate(flops=1 << 16, bytes_accessed=1 << 16, transcendentals=0),
    )(place, attended, residual, gain, ids, scores)


def chosen(ranks, slots):
    slot = lax.broadcasted_iota(jnp.int32, (slots, ranks.shape[1]), 0)
    return (slot.astype(f32) == ranks).astype(bf16)


def list_kernel(place, own, other, onehots, stats, share, ranks):
    y, first = place[0], place[1]
    experts, rows, slots = onehots.shape
    parts, extra = stats.shape[0], own.shape[1]
    notes = jnp.concatenate([own[...], other[...]], axis=0).astype(f32)
    named = notes > 0.0
    before = lax.broadcasted_iota(jnp.int32, (rows, rows), 1) <= lax.broadcasted_iota(
        jnp.int32, (rows, rows), 0
    )
    counts = jnp.dot(
        before.astype(bf16), jnp.where(named, 1.0, 0.0).astype(bf16), preferred_element_type=f32
    )
    placed = jnp.where(named, counts - 1.0, -1.0)
    column = lax.broadcasted_iota(jnp.int32, (rows, extra), 1)
    slot = lax.broadcasted_iota(jnp.int32, (rows, slots), 1).astype(f32)
    ranks[...] = jnp.transpose(placed)
    turned = jnp.transpose(notes)[: 2 * EXPERTS].astype(bf16)
    line = lax.broadcasted_iota(jnp.int32, (2 * EXPERTS, slots), 0)
    for e in range(experts):
        rank = jnp.sum(jnp.where(column == first + e, placed, 0.0), axis=1, keepdims=True)
        onehot = (slot == rank).astype(bf16)
        onehots[e] = onehot
        listed = jnp.dot(turned, onehot, preferred_element_type=f32)
        for h in range(parts // experts):
            stats[e * (parts // experts) + h] = listed[EXPERTS:]

        @pl.when(y // (parts // experts) == e)
        def _():
            values = jnp.sum(jnp.where(line == first + e, listed, 0.0), axis=0, keepdims=True)
            share[...] = jnp.broadcast_to(values, share.shape)


def list_rows(place, own, other, experts, parts):
    rows, extra = 2 * own.shape[0], own.shape[1]
    slots = rows * CAPACITY_OF_512 // 512
    whole = pl.BlockSpec(memory_space=VMEM)
    return pl.pallas_call(
        list_kernel,
        out_shape=[
            jax.ShapeDtypeStruct((experts, rows, slots), bf16),
            jax.ShapeDtypeStruct((parts, EXPERTS, slots), f32),
            jax.ShapeDtypeStruct((EXPERTS, slots), f32),
            jax.ShapeDtypeStruct((extra, rows), f32),
        ],
        in_specs=[pl.BlockSpec(memory_space=SMEM)] + [whole] * 2,
        out_specs=[whole] * 4,
        compiler_params=pltpu.CompilerParams(vmem_limit_bytes=12 << 20),
        cost_estimate=pl.CostEstimate(flops=1 << 27, bytes_accessed=1 << 20, transcendentals=0),
    )(place, own, other)


def pack_kernel(place, own, other, onehots, below, *outs):
    experts, fan, _ = own.shape
    units = outs[0].shape[0] - below.shape[1]
    for e in range(experts):
        packed = jnp.concatenate([own[e], other[e]], axis=1)
        packed = jnp.dot(packed, onehots[e], preferred_element_type=f32)
        for h in range(fan // units):
            q = e * (fan // units) + h
            part = jnp.concatenate([packed[h * units : (h + 1) * units], below[q]], axis=0)
            part = part.astype(bf16)
            step = lax.rem(q + len(outs) - place[0], len(outs))
            for k, out in enumerate(outs):

                @pl.when(step == k)
                def _(out=out, part=part):
                    out[...] = part


def pack(place, own, other, onehots, below):
    experts, fan, _ = own.shape
    parts, lines, slots = below.shape
    whole = pl.BlockSpec(memory_space=VMEM)
    return pl.pallas_call(
        pack_kernel,
        out_shape=[jax.ShapeDtypeStruct((experts * fan // parts + lines, slots), bf16)] * parts,
        in_specs=[pl.BlockSpec(memory_space=SMEM)] + [whole] * 4,
        out_specs=[whole] * parts,
        compiler_params=pltpu.CompilerParams(vmem_limit_bytes=12 << 20),
        cost_estimate=pl.CostEstimate(flops=1 << 28, bytes_accessed=2 << 20, transcendentals=0),
    )(place, own, other, onehots, below)


def split_kernel(*refs):
    *pieces, rows, features, routes = refs
    width, at = features.shape[1], 0
    for piece in pieces:
        count = piece.shape[0]
        if rows is not None:
            rows[at : at + count] = piece[...]
        features[at : at + count] = piece[:, :width]
        routes[at : at + count] = piece[:, width:]
        at += count


def split(pieces, width, joined):
    count, columns = sum(p.shape[0] for p in pieces), pieces[0].shape[1]
    whole = pl.BlockSpec(memory_space=VMEM)
    widths = [columns] * joined + [width, columns - width]

    def kernel(*refs):
        outs = refs[len(pieces) :]
        split_kernel(*refs[: len(pieces)], outs[0] if joined else None, *outs[-2:])

    return pl.pallas_call(
        kernel,
        out_shape=[jax.ShapeDtypeStruct((count, w), pieces[0].dtype) for w in widths],
        in_specs=[whole] * len(pieces),
        out_specs=[whole] * len(widths),
        compiler_params=pltpu.CompilerParams(vmem_limit_bytes=8 << 20),
        cost_estimate=pl.CostEstimate(flops=1, bytes_accessed=1 << 20, transcendentals=0),
    )(*pieces)


def activate_kernel(*refs):
    *parts, share, hidden = refs
    half = len(parts) // 2
    parts = [[p[...].astype(f32) for p in pair] for pair in zip(parts[:half], parts[half:])]
    units, slots = hidden.shape
    count = len(parts)
    means, devs = [], []
    for part in parts:
        stats = part[0][units:]
        means.append(stats[0:1] + stats[1:2] + stats[2:3])
        devs.append(stats[3:4] + stats[4:5] + stats[5:6])
    mean = sum(means) / count
    var = sum(devs) / (count * PART_WIDTH)
    var = var + sum(jnp.square(m - mean) for m in means) / count
    scale = lax.rsqrt(var + epsilon)
    gains = []
    for part in parts:
        terms = part[1][units:]
        gains += [terms[0:1] + terms[1:2] + terms[2:3], terms[3:4] + terms[4:5] + terms[5:6]]
    columns = jnp.transpose(jnp.concatenate(gains, axis=0)[:, :256])[:units]

    def total(g):
        result = sum(part[g][:units] for part in parts)
        for k in range(count):
            result = result + columns[:, 2 * k + g : 2 * k + g + 1] * (means[k] - mean)
        return result * scale

    gate = total(0)
    hidden[...] = (gate * jax.nn.sigmoid(gate) * total(1) * share[0:1]).astype(bf16)


def activate(parts, share):
    whole = pl.BlockSpec(memory_space=VMEM)
    units, slots = parts[0].shape[0] - EXPERTS, parts[0].shape[1]
    return pl.pallas_call(
        activate_kernel,
        out_shape=jax.ShapeDtypeStruct((units, slots), bf16),
        in_specs=[whole] * (len(parts) + 1),
        out_specs=whole,
        compiler_params=pltpu.CompilerParams(vmem_limit_bytes=8 << 20),
        cost_estimate=pl.CostEstimate(flops=1, bytes_accessed=1 << 20, transcendentals=1),
    )(*parts, share)


def scatter_kernel(place, hidden0, hidden1, hidden2, hidden3, ranks, out):
    parts, slots = out.shape[0], hidden0.shape[1]
    for k, hidden in enumerate((hidden0, hidden1, hidden2, hidden3)):
        at = lax.rem(place[0] + k, parts)
        onehot = chosen(ranks[pl.ds(place[1] + at // 2, 1), :], slots)
        out[at] = jnp.dot(hidden[...], onehot, preferred_element_type=f32).astype(bf16)


def scatter(place, hidden, ranks):
    whole = pl.BlockSpec(memory_space=VMEM)
    return pl.pallas_call(
        scatter_kernel,
        out_shape=jax.ShapeDtypeStruct((4, hidden[0].shape[0], ranks.shape[1]), bf16),
        in_specs=[pl.BlockSpec(memory_space=SMEM)] + [whole] * 5,
        out_specs=whole,
        compiler_params=pltpu.CompilerParams(vmem_limit_bytes=16 << 20),
        cost_estimate=pl.CostEstimate(flops=1 << 28, bytes_accessed=1 << 20, transcendentals=0),
    )(place, *hidden, ranks)


def per_device(
    queries,
    cache_keys,
    stored_values,
    lengths,
    residual_in,
    norm_gain,
    expert_ids,
    expert_scores,
    w_gate,
    w_up,
    w_down,
):
    y, x = lax.axis_index("etp"), lax.axis_index("egrp")
    y_size = lax.axis_size("etp")
    attended = attend(queries, cache_keys, stored_values, lengths)
    place = jnp.stack([y, x * w_gate.shape[0]]).astype(jnp.int32)
    stream, held = finish(place, attended, residual_in, norm_gain, expert_ids.T, expert_scores.T)
    rows, width = stream.shape
    gain = lax.dynamic_slice_in_dim(norm_gain, y * width, width, 0).astype(f32)

    units = w_gate.shape[0] * w_gate.shape[2] // y_size
    down = w_down.reshape(-1, width)

    def project(weight, tokens):
        return jnp.einsum("edf,rd->efr", weight, tokens, preferred_element_type=f32).astype(bf16)

    across = along_z(held, 4)
    chip = jnp.concatenate([held, swap_core(held)], axis=0)
    held = jnp.concatenate([held, across] + [along_z(chip, k) for k in (1, 2, 3)], axis=0)
    gain, held = lax.optimization_barrier((gain, held))
    gains = jnp.stack(
        [jnp.einsum("edf,d->ef", w.astype(f32), gain).reshape(y_size, -1) for w in (w_gate, w_up)]
    )

    terms, rest = [], gains
    for _ in range(3):
        terms.append(lax.reduce_precision(rest, 8, 7))
        rest = rest - terms[-1]
    gains = jnp.stack(terms, axis=1).reshape(2 * len(terms), y_size, units).swapaxes(0, 1)
    slots = 4 * held.shape[0] * 2 * CAPACITY_OF_512 // 512
    gains = jnp.pad(gains, ((0, 0), (0, EXPERTS - gains.shape[1]), (0, slots - units)))
    pieces = [along_x(held, k) for k in range(3)]
    pieces, gains = lax.optimization_barrier((pieces, gains))
    own, own_rows, own_notes = split([held] + pieces, width, True)
    other_rows, other_notes = split([swap_core(own)], width, False)
    onehots, stats, share, ranks = list_rows(
        place, own_notes, other_notes, w_gate.shape[0], y_size
    )
    gate_sums, up_sums = project(w_gate, own_rows), project(w_up, own_rows)
    gate_parts = pack(place, gate_sums, project(w_gate, other_rows), onehots, stats)
    other_rows, gate_parts = lax.optimization_barrier((other_rows, gate_parts))
    up_parts = pack(place, up_sums, project(w_up, other_rows), onehots, gains)
    parts = []
    for packed in (gate_parts, up_parts):
        parts += [packed[0]] + [to_y(packed[k], k) for k in range(1, y_size)]
    hidden = activate(parts, share)
    got = {k: to_y(hidden, -k) for k in (1, 3, 2)}
    hidden = scatter(place, [hidden] + [got[k] for k in range(1, y_size)], ranks)
    hidden = hidden.reshape(down.shape[0], -1)
    n = own.shape[0]

    def back_down(at):
        return jnp.einsum("fr,fd->rd", hidden[:, at : at + n], down, preferred_element_type=f32)

    other = swap_core(back_down(n).astype(bf16))
    total = lax.optimization_barrier(back_down(0)) + other.astype(f32)
    n = n // 4
    total, sent = lax.optimization_barrier(
        (total[:n], [total[k * n : (k + 1) * n].astype(bf16) for k in range(1, 4)])
    )
    total = total + sum(along_x(sent[k], k).astype(f32) for k in range(3))
    n = 2 * rows
    mine, across, *chip = lax.optimization_barrier(
        (total[:rows], total[rows:n].astype(bf16))
        + tuple(total[k * n : (k + 1) * n].astype(bf16) for k in (1, 2, 3))
    )
    chip = sum(along_z(part, k + 1, True).astype(f32) for k, part in enumerate(chip))
    mine = mine + along_z(across, 4, True).astype(f32) + chip[:rows]
    mine = mine + swap_core(chip[rows:].astype(bf16)).astype(f32)
    return (stream, mine.astype(bf16))


def solution(mesh):
    placed = (
        P(("attn", "egrp"), "etp"),
        P(("attn", "egrp"), None, "etp"),
        P(("attn", "egrp"), None, "etp"),
        P(("attn", "egrp")),
        P(("attn", "egrp"), "etp"),
        P(),
        P(("attn", "egrp"), None),
        P(("attn", "egrp"), None),
        P("egrp", "etp", "attn"),
        P("egrp", "etp", "attn"),
        P("egrp", "attn", "etp"),
    )
    return jax.shard_map(
        per_device,
        mesh=mesh,
        in_specs=placed,
        out_specs=(P(("attn", "egrp"), "etp"), P(("attn", "egrp"), "etp")),
        check_vma=False,
    )
```

```python
import math

import jax
import jax.numpy as jnp
from jax import lax
from jax.experimental import pallas as pl
from jax.experimental.pallas import tpu as pltpu
from jax.sharding import PartitionSpec as P

HEAD_SIZE = 128
EXPERTS = 8

epsilon = 1e-05
PART_WIDTH = 1536
f32, bf16 = jnp.float32, jnp.bfloat16


def attend(queries, cache_keys, stored_values, lengths):
    row_count = queries.shape[0]
    span = cache_keys.shape[1]
    kv_heads = cache_keys.shape[2] // HEAD_SIZE
    query_group = queries.shape[1] // (kv_heads * HEAD_SIZE)
    query_blocks = queries.reshape(row_count, kv_heads, query_group, HEAD_SIZE)
    key_blocks = cache_keys.reshape(row_count, span, kv_heads, HEAD_SIZE)
    value_blocks = stored_values.reshape(row_count, span, kv_heads, HEAD_SIZE)
    scores = jnp.einsum(
        "rhgd,rlhd->rhgl", query_blocks, key_blocks, preferred_element_type=f32
    ) * (1.0 / math.sqrt(HEAD_SIZE))
    position = lax.broadcasted_iota(jnp.int32, scores.shape, 3)
    visible = position < jnp.broadcast_to(lengths[:, None, None, None], scores.shape)
    scores = jnp.where(visible, scores, -1e30)
    peak = jnp.max(scores, axis=-1, keepdims=True)
    expd = jnp.exp(scores - peak)
    totals = jnp.sum(expd, axis=-1, keepdims=True)
    weights_bf = (expd / totals).astype(bf16)
    attended = jnp.einsum(
        "rhgl,rlhd->rhgd", weights_bf, value_blocks, preferred_element_type=f32
    )
    return attended.reshape(row_count, kv_heads * query_group * HEAD_SIZE)


def send(x, axes, target):
    sizes = [lax.axis_size(axis) for axis in axes]
    pairs = []
    for index in range(math.prod(sizes)):
        place, rest = [], index
        for size in reversed(sizes):
            place.insert(0, rest % size)
            rest //= size
        other = 0
        for coordinate, size in zip(target(*place), sizes):
            other = other * size + coordinate % size
        pairs.append((index, other))
    return lax.ppermute(x, axes, pairs)


def swap_core(x):
    return send(x, ("attn",), lambda a: (a ^ 1,))


def along_z(x, step, back=False):
    sign = 1 if back else -1
    return send(x, ("attn",), lambda a: (a + sign * 2 * (step if a % 2 == 0 else -step),))


def along_x(x, step):
    return send(x, ("attn", "egrp"), lambda a, i: (a, i ^ (2 if step == 2 else 1 if a % 2 == step else 3)))


def to_y(x, step):
    return send(x, ("etp",), lambda i: (i + step,))


VMEM, SMEM, ANY = pltpu.VMEM, pltpu.SMEM, pl.ANY
NT = (((1,), (1,)), ((), ()))
CAPACITY_OF_512 = 384


def finish_kernel(place, attended, residual, gain, ids, scores, stream, held):
    rows, width = attended.shape
    column = lax.broadcasted_iota(jnp.int32, (rows, held.shape[1] - width), 1)
    share = scores[...] / jnp.sum(scores[...], axis=0, keepdims=True)
    share, named = jnp.transpose(share), jnp.transpose(ids[...].astype(f32))
    notes = jnp.zeros(column.shape, f32)
    for k in range(named.shape[1]):
        here = column.astype(f32) == named[:, k : k + 1]
        notes = notes + jnp.where(here, share[:, k : k + 1], 0.0)
    summed = residual[...].astype(f32) + attended[...].astype(bf16).astype(f32)
    stream[...] = summed.astype(bf16)
    raw = summed.astype(bf16).astype(f32)
    mean = jnp.sum(raw, axis=1, keepdims=True) / width
    centred = raw - mean
    dev = jnp.sum(jnp.square(centred), axis=1, keepdims=True)
    at = EXPERTS
    for rest in (mean, dev):
        for _ in range(3):
            term = rest.astype(bf16).astype(f32)
            notes = jnp.where(column == at, term, notes)
            rest, at = rest - term, at + 1
    own = gain[pl.ds(pl.multiple_of(place[0] * width, width), width)]
    held[:, :width] = (centred * own.astype(f32).reshape(1, width)).astype(bf16)
    held[:, width:] = notes.astype(bf16)


def finish(place, attended, residual, gain, ids, scores):
    whole = pl.BlockSpec(memory_space=VMEM)
    rows, width = attended.shape
    return pl.pallas_call(
        finish_kernel,
        out_shape=[
            jax.ShapeDtypeStruct((rows, width), bf16),
            jax.ShapeDtypeStruct((rows, width + 128), bf16),
        ],
        in_specs=[pl.BlockSpec(memory_space=SMEM)] + [whole] * 5,
        out_specs=[whole] * 2,
        compiler_params=pltpu.CompilerParams(vmem_limit_bytes=4 << 20),
        cost_estimate=pl.CostEstimate(flops=1 << 16, bytes_accessed=1 << 16, transcendentals=0),
    )(place, attended, residual, gain, ids, scores)


def chosen(ranks, slots):
    slot = lax.broadcasted_iota(jnp.int32, (slots, ranks.shape[1]), 0)
    return (slot.astype(f32) == ranks).astype(bf16)


def list_kernel(place, own, other, onehots, stats, share, ranks):
    y, first = place[0], place[1]
    experts, rows, slots = onehots.shape
    parts, extra = stats.shape[0], own.shape[1]
    notes = jnp.concatenate([own[...], other[...]], axis=0).astype(f32)
    named = notes > 0.0
    before = lax.broadcasted_iota(jnp.int32, (rows, rows), 1) <= lax.broadcasted_iota(
        jnp.int32, (rows, rows), 0
    )
    counts = jnp.dot(
        before.astype(bf16), jnp.where(named, 1.0, 0.0).astype(bf16), preferred_element_type=f32
    )
    placed = jnp.where(named, counts - 1.0, -1.0)
    column = lax.broadcasted_iota(jnp.int32, (rows, extra), 1)
    slot = lax.broadcasted_iota(jnp.int32, (rows, slots), 1).astype(f32)
    ranks[...] = jnp.transpose(placed)
    turned = jnp.transpose(notes)[: 2 * EXPERTS].astype(bf16)
    line = lax.broadcasted_iota(jnp.int32, (2 * EXPERTS, slots), 0)
    for e in range(experts):
        rank = jnp.sum(jnp.where(column == first + e, placed, 0.0), axis=1, keepdims=True)
        onehot = (slot == rank).astype(bf16)
        onehots[e] = onehot
        listed = jnp.dot(turned, onehot, preferred_element_type=f32)
        for h in range(parts // experts):
            stats[e * (parts // experts) + h] = listed[EXPERTS:]

        @pl.when(y // (parts // experts) == e)
        def _():
            values = jnp.sum(jnp.where(line == first + e, listed, 0.0), axis=0, keepdims=True)
            share[...] = jnp.broadcast_to(values, share.shape)


def list_rows(place, own, other, experts, parts):
    rows, extra = 2 * own.shape[0], own.shape[1]
    slots = rows * CAPACITY_OF_512 // 512
    whole = pl.BlockSpec(memory_space=VMEM)
    return pl.pallas_call(
        list_kernel,
        out_shape=[
            jax.ShapeDtypeStruct((experts, rows, slots), bf16),
            jax.ShapeDtypeStruct((parts, EXPERTS, slots), f32),
            jax.ShapeDtypeStruct((EXPERTS, slots), f32),
            jax.ShapeDtypeStruct((extra, rows), f32),
        ],
        in_specs=[pl.BlockSpec(memory_space=SMEM)] + [whole] * 2,
        out_specs=[whole] * 4,
        compiler_params=pltpu.CompilerParams(vmem_limit_bytes=12 << 20),
        cost_estimate=pl.CostEstimate(flops=1 << 27, bytes_accessed=1 << 20, transcendentals=0),
    )(place, own, other)


def pack_kernel(place, own, other, onehots, below, *outs):
    experts, fan, _ = own.shape
    units = outs[0].shape[0] - below.shape[1]
    for e in range(experts):
        packed = jnp.concatenate([own[e], other[e]], axis=1)
        packed = jnp.dot(packed, onehots[e], preferred_element_type=f32)
        for h in range(fan // units):
            q = e * (fan // units) + h
            part = jnp.concatenate([packed[h * units : (h + 1) * units], below[q]], axis=0)
            part = part.astype(bf16)
            step = lax.rem(q + len(outs) - place[0], len(outs))
            for k, out in enumerate(outs):

                @pl.when(step == k)
                def _(out=out, part=part):
                    out[...] = part


def pack(place, own, other, onehots, below):
    experts, fan, _ = own.shape
    parts, lines, slots = below.shape
    whole = pl.BlockSpec(memory_space=VMEM)
    return pl.pallas_call(
        pack_kernel,
        out_shape=[jax.ShapeDtypeStruct((experts * fan // parts + lines, slots), bf16)] * parts,
        in_specs=[pl.BlockSpec(memory_space=SMEM)] + [whole] * 4,
        out_specs=[whole] * parts,
        compiler_params=pltpu.CompilerParams(vmem_limit_bytes=12 << 20),
        cost_estimate=pl.CostEstimate(flops=1 << 28, bytes_accessed=2 << 20, transcendentals=0),
    )(place, own, other, onehots, below)


def split_kernel(*refs):
    *pieces, rows, features, routes = refs
    width, at = features.shape[1], 0
    for piece in pieces:
        count = piece.shape[0]
        if rows is not None:
            rows[at : at + count] = piece[...]
        features[at : at + count] = piece[:, :width]
        routes[at : at + count] = piece[:, width:]
        at += count


def split(pieces, width, joined):
    count, columns = sum(p.shape[0] for p in pieces), pieces[0].shape[1]
    whole = pl.BlockSpec(memory_space=VMEM)
    widths = [columns] * joined + [width, columns - width]

    def kernel(*refs):
        outs = refs[len(pieces) :]
        split_kernel(*refs[: len(pieces)], outs[0] if joined else None, *outs[-2:])

    return pl.pallas_call(
        kernel,
        out_shape=[jax.ShapeDtypeStruct((count, w), pieces[0].dtype) for w in widths],
        in_specs=[whole] * len(pieces),
        out_specs=[whole] * len(widths),
        compiler_params=pltpu.CompilerParams(vmem_limit_bytes=8 << 20),
        cost_estimate=pl.CostEstimate(flops=1, bytes_accessed=1 << 20, transcendentals=0),
    )(*pieces)


def activate_kernel(*refs):
    *parts, share, hidden = refs
    half = len(parts) // 2
    parts = [[p[...].astype(f32) for p in pair] for pair in zip(parts[:half], parts[half:])]
    units, slots = hidden.shape
    count = len(parts)
    means, devs = [], []
    for part in parts:
        stats = part[0][units:]
        means.append(stats[0:1] + stats[1:2] + stats[2:3])
        devs.append(stats[3:4] + stats[4:5] + stats[5:6])
    mean = sum(means) / count
    var = sum(devs) / (count * PART_WIDTH)
    var = var + sum(jnp.square(m - mean) for m in means) / count
    scale = lax.rsqrt(var + epsilon)
    gains = []
    for part in parts:
        terms = part[1][units:]
        gains += [terms[0:1] + terms[1:2] + terms[2:3], terms[3:4] + terms[4:5] + terms[5:6]]
    columns = jnp.transpose(jnp.concatenate(gains, axis=0)[:, :256])[:units]

    def total(g):
        result = sum(part[g][:units] for part in parts)
        for k in range(count):
            result = result + columns[:, 2 * k + g : 2 * k + g + 1] * (means[k] - mean)
        return result * scale

    gate = total(0)
    hidden[...] = (gate * jax.nn.sigmoid(gate) * total(1) * share[0:1]).astype(bf16)


def activate(parts, share):
    whole = pl.BlockSpec(memory_space=VMEM)
    units, slots = parts[0].shape[0] - EXPERTS, parts[0].shape[1]
    return pl.pallas_call(
        activate_kernel,
        out_shape=jax.ShapeDtypeStruct((units, slots), bf16),
        in_specs=[whole] * (len(parts) + 1),
        out_specs=whole,
        compiler_params=pltpu.CompilerParams(vmem_limit_bytes=8 << 20),
        cost_estimate=pl.CostEstimate(flops=1, bytes_accessed=1 << 20, transcendentals=1),
    )(*parts, share)


def scatter_kernel(place, hidden0, hidden1, hidden2, hidden3, ranks, out):
    parts, slots = out.shape[0], hidden0.shape[1]
    for k, hidden in enumerate((hidden0, hidden1, hidden2, hidden3)):
        at = lax.rem(place[0] + k, parts)
        onehot = chosen(ranks[pl.ds(place[1] + at // 2, 1), :], slots)
        out[at] = jnp.dot(hidden[...], onehot, preferred_element_type=f32).astype(bf16)


def scatter(place, hidden, ranks):
    whole = pl.BlockSpec(memory_space=VMEM)
    return pl.pallas_call(
        scatter_kernel,
        out_shape=jax.ShapeDtypeStruct((4, hidden[0].shape[0], ranks.shape[1]), bf16),
        in_specs=[pl.BlockSpec(memory_space=SMEM)] + [whole] * 5,
        out_specs=whole,
        compiler_params=pltpu.CompilerParams(vmem_limit_bytes=16 << 20),
        cost_estimate=pl.CostEstimate(flops=1 << 28, bytes_accessed=1 << 20, transcendentals=0),
    )(place, *hidden, ranks)


def per_device(
    queries,
    cache_keys,
    stored_values,
    lengths,
    residual_in,
    norm_gain,
    expert_ids,
    expert_scores,
    w_gate,
    w_up,
    w_down,
):
    y, x = lax.axis_index("etp"), lax.axis_index("egrp")
    y_size = lax.axis_size("etp")
    attended = attend(queries, cache_keys, stored_values, lengths)
    place = jnp.stack([y, x * w_gate.shape[0]]).astype(jnp.int32)
    stream, held = finish(place, attended, residual_in, norm_gain, expert_ids.T, expert_scores.T)
    rows, width = stream.shape
    gain = lax.dynamic_slice_in_dim(norm_gain, y * width, width, 0).astype(f32)

    units = w_gate.shape[0] * w_gate.shape[2] // y_size
    down = w_down.reshape(-1, width)

    def project(weight, tokens):
        return jnp.einsum("edf,rd->efr", weight, tokens, preferred_element_type=f32).astype(bf16)

    across = along_z(held, 4)
    chip = jnp.concatenate([held, swap_core(held)], axis=0)
    held = jnp.concatenate([held, across] + [along_z(chip, k) for k in (1, 2, 3)], axis=0)
    gain, held = lax.optimization_barrier((gain, held))
    gains = jnp.stack(
        [jnp.einsum("edf,d->ef", w.astype(f32), gain).reshape(y_size, -1) for w in (w_gate, w_up)]
    )

    terms, rest = [], gains
    for _ in range(3):
        terms.append(lax.reduce_precision(rest, 8, 7))
        rest = rest - terms[-1]
    gains = jnp.stack(terms, axis=1).reshape(2 * len(terms), y_size, units).swapaxes(0, 1)
    slots = 4 * held.shape[0] * 2 * CAPACITY_OF_512 // 512
    gains = jnp.pad(gains, ((0, 0), (0, EXPERTS - gains.shape[1]), (0, slots - units)))
    pieces = [along_x(held, k) for k in range(3)]
    pieces, gains = lax.optimization_barrier((pieces, gains))
    own, own_rows, own_notes = split([held] + pieces, width, True)
    other_rows, other_notes = split([swap_core(own)], width, False)
    onehots, stats, share, ranks = list_rows(
        place, own_notes, other_notes, w_gate.shape[0], y_size
    )
    gate_sums = [project(w_gate, r) for r in (own_rows, other_rows)]
    gate_parts = pack(place, *gate_sums, onehots, stats)
    own_rows, other_rows, gate_parts = lax.optimization_barrier((own_rows, other_rows, gate_parts))
    up_sums = [project(w_up, r) for r in (own_rows, other_rows)]
    up_parts = pack(place, *up_sums, onehots, gains)
    parts = []
    for packed in (gate_parts, up_parts):
        parts += [packed[0]] + [to_y(packed[k], k) for k in range(1, y_size)]
    hidden = activate(parts, share)
    got = {k: to_y(hidden, -k) for k in (1, 3, 2)}
    hidden = scatter(place, [hidden] + [got[k] for k in range(1, y_size)], ranks)
    hidden = hidden.reshape(down.shape[0], -1)
    n = own.shape[0] // 4

    def over_cores(hidden, first, last):
        def output(at):
            part = hidden[:, at + first * n : at + last * n]
            return jnp.einsum("fr,fd->rd", part, down, preferred_element_type=f32)

        other = swap_core(output(4 * n).astype(bf16))
        return lax.optimization_barrier(output(0)) + other.astype(f32)

    distant = over_cores(hidden, 3, 4).astype(bf16)
    distant, hidden = lax.optimization_barrier((distant, hidden))
    total = over_cores(hidden, 0, 3)
    total, *sent = lax.optimization_barrier(
        (total[:n], total[n : 2 * n].astype(bf16), total[2 * n :].astype(bf16))
    )
    got = [along_x(part, k) for k, part in enumerate(sent + [distant])]
    total = total + sum(part.astype(f32) for part in got)
    n = 2 * rows
    mine, across, *chip = lax.optimization_barrier(
        (total[:rows], total[rows:n].astype(bf16))
        + tuple(total[k * n : (k + 1) * n].astype(bf16) for k in (1, 2, 3))
    )
    chip = sum(along_z(part, k + 1, True).astype(f32) for k, part in enumerate(chip))
    mine = mine + along_z(across, 4, True).astype(f32) + chip[:rows]
    mine = mine + swap_core(chip[rows:].astype(bf16)).astype(f32)
    return (stream, mine.astype(bf16))


def solution(mesh):
    placed = (
        P(("attn", "egrp"), "etp"),
        P(("attn", "egrp"), None, "etp"),
        P(("attn", "egrp"), None, "etp"),
        P(("attn", "egrp")),
        P(("attn", "egrp"), "etp"),
        P(),
        P(("attn", "egrp"), None),
        P(("attn", "egrp"), None),
        P("egrp", "etp", "attn"),
        P("egrp", "etp", "attn"),
        P("egrp", "attn", "etp"),
    )
    return jax.shard_map(
        per_device,
        mesh=mesh,
        in_specs=placed,
        out_specs=(P(("attn", "egrp"), "etp"), P(("attn", "egrp"), "etp")),
        check_vma=False,
    )
```

```python
import math

import jax
import jax.numpy as jnp
from jax import lax
from jax.experimental import pallas as pl
from jax.experimental.pallas import tpu as pltpu
from jax.sharding import PartitionSpec as P

HEAD_SIZE = 128
EXPERTS = 8

epsilon = 1e-05
PART_WIDTH = 1536
f32, bf16 = jnp.float32, jnp.bfloat16


def attend(queries, cache_keys, stored_values, lengths):
    row_count = queries.shape[0]
    span = cache_keys.shape[1]
    kv_heads = cache_keys.shape[2] // HEAD_SIZE
    query_group = queries.shape[1] // (kv_heads * HEAD_SIZE)
    query_blocks = queries.reshape(row_count, kv_heads, query_group, HEAD_SIZE)
    key_blocks = cache_keys.reshape(row_count, span, kv_heads, HEAD_SIZE)
    value_blocks = stored_values.reshape(row_count, span, kv_heads, HEAD_SIZE)
    scores = jnp.einsum(
        "rhgd,rlhd->rhgl", query_blocks, key_blocks, preferred_element_type=f32
    ) * (1.0 / math.sqrt(HEAD_SIZE))
    position = lax.broadcasted_iota(jnp.int32, scores.shape, 3)
    visible = position < jnp.broadcast_to(lengths[:, None, None, None], scores.shape)
    scores = jnp.where(visible, scores, -1e30)
    peak = jnp.max(scores, axis=-1, keepdims=True)
    expd = jnp.exp(scores - peak)
    totals = jnp.sum(expd, axis=-1, keepdims=True)
    weights_bf = (expd / totals).astype(bf16)
    attended = jnp.einsum(
        "rhgl,rlhd->rhgd", weights_bf, value_blocks, preferred_element_type=f32
    )
    return attended.reshape(row_count, kv_heads * query_group * HEAD_SIZE)


def send(x, axes, target):
    sizes = [lax.axis_size(axis) for axis in axes]
    pairs = []
    for index in range(math.prod(sizes)):
        place, rest = [], index
        for size in reversed(sizes):
            place.insert(0, rest % size)
            rest //= size
        other = 0
        for coordinate, size in zip(target(*place), sizes):
            other = other * size + coordinate % size
        pairs.append((index, other))
    return lax.ppermute(x, axes, pairs)


def swap_core(x):
    return send(x, ("attn",), lambda a: (a ^ 1,))


def along_z(x, step, back=False):
    sign = 1 if back else -1
    return send(x, ("attn",), lambda a: (a + sign * 2 * (step if a % 2 == 0 else -step),))


def along_x(x, step):
    return send(x, ("attn", "egrp"), lambda a, i: (a, i ^ (2 if step == 2 else 1 if a % 2 == step else 3)))


def to_y(x, step):
    return send(x, ("etp",), lambda i: (i + step,))


VMEM, SMEM, ANY = pltpu.VMEM, pltpu.SMEM, pl.ANY
NT = (((1,), (1,)), ((), ()))
CAPACITY_OF_512 = 384


def finish_kernel(place, attended, residual, gain, ids, scores, stream, held):
    rows, width = attended.shape
    column = lax.broadcasted_iota(jnp.int32, (rows, held.shape[1] - width), 1)
    share = scores[...] / jnp.sum(scores[...], axis=0, keepdims=True)
    share, named = jnp.transpose(share), jnp.transpose(ids[...].astype(f32))
    notes = jnp.zeros(column.shape, f32)
    for k in range(named.shape[1]):
        here = column.astype(f32) == named[:, k : k + 1]
        notes = notes + jnp.where(here, share[:, k : k + 1], 0.0)
    summed = residual[...].astype(f32) + attended[...].astype(bf16).astype(f32)
    stream[...] = summed.astype(bf16)
    raw = summed.astype(bf16).astype(f32)
    mean = jnp.sum(raw, axis=1, keepdims=True) / width
    centred = raw - mean
    dev = jnp.sum(jnp.square(centred), axis=1, keepdims=True)
    at = EXPERTS
    for rest in (mean, dev):
        for _ in range(3):
            term = rest.astype(bf16).astype(f32)
            notes = jnp.where(column == at, term, notes)
            rest, at = rest - term, at + 1
    own = gain[pl.ds(pl.multiple_of(place[0] * width, width), width)]
    held[:, :width] = (centred * own.astype(f32).reshape(1, width)).astype(bf16)
    held[:, width:] = notes.astype(bf16)


def finish(place, attended, residual, gain, ids, scores):
    whole = pl.BlockSpec(memory_space=VMEM)
    rows, width = attended.shape
    return pl.pallas_call(
        finish_kernel,
        out_shape=[
            jax.ShapeDtypeStruct((rows, width), bf16),
            jax.ShapeDtypeStruct((rows, width + 128), bf16),
        ],
        in_specs=[pl.BlockSpec(memory_space=SMEM)] + [whole] * 5,
        out_specs=[whole] * 2,
        compiler_params=pltpu.CompilerParams(vmem_limit_bytes=4 << 20),
        cost_estimate=pl.CostEstimate(flops=1 << 16, bytes_accessed=1 << 16, transcendentals=0),
    )(place, attended, residual, gain, ids, scores)


def chosen(ranks, slots):
    slot = lax.broadcasted_iota(jnp.int32, (slots, ranks.shape[1]), 0)
    return (slot.astype(f32) == ranks).astype(bf16)


def list_kernel(place, own, other, onehots, stats, share, ranks):
    y, first = place[0], place[1]
    experts, rows, slots = onehots.shape
    parts, extra = stats.shape[0], own.shape[1]
    notes = jnp.concatenate([own[...], other[...]], axis=0).astype(f32)
    named = notes > 0.0
    before = lax.broadcasted_iota(jnp.int32, (rows, rows), 1) <= lax.broadcasted_iota(
        jnp.int32, (rows, rows), 0
    )
    counts = jnp.dot(
        before.astype(bf16), jnp.where(named, 1.0, 0.0).astype(bf16), preferred_element_type=f32
    )
    placed = jnp.where(named, counts - 1.0, -1.0)
    column = lax.broadcasted_iota(jnp.int32, (rows, extra), 1)
    slot = lax.broadcasted_iota(jnp.int32, (rows, slots), 1).astype(f32)
    turned = jnp.transpose(notes)[: 2 * EXPERTS]
    listing = turned > 0.0
    counts = lax.dot_general(
        jnp.where(listing, 1.0, 0.0).astype(bf16), before.astype(bf16), NT, preferred_element_type=f32
    )
    ranks[...] = jnp.where(listing, counts - 1.0, -1.0)
    turned = turned.astype(bf16)
    line = lax.broadcasted_iota(jnp.int32, (2 * EXPERTS, slots), 0)
    for e in range(experts):
        rank = jnp.sum(jnp.where(column == first + e, placed, 0.0), axis=1, keepdims=True)
        onehot = (slot == rank).astype(bf16)
        onehots[e] = onehot
        listed = jnp.dot(turned, onehot, preferred_element_type=f32)
        for h in range(parts // experts):
            stats[e * (parts // experts) + h] = listed[EXPERTS:]

        @pl.when(y // (parts // experts) == e)
        def _():
            values = jnp.sum(jnp.where(line == first + e, listed, 0.0), axis=0, keepdims=True)
            share[...] = jnp.broadcast_to(values, share.shape)


def list_rows(place, own, other, experts, parts):
    rows = 2 * own.shape[0]
    slots = rows * CAPACITY_OF_512 // 512
    whole = pl.BlockSpec(memory_space=VMEM)
    return pl.pallas_call(
        list_kernel,
        out_shape=[
            jax.ShapeDtypeStruct((experts, rows, slots), bf16),
            jax.ShapeDtypeStruct((parts, EXPERTS, slots), f32),
            jax.ShapeDtypeStruct((EXPERTS, slots), f32),
            jax.ShapeDtypeStruct((2 * EXPERTS, rows), f32),
        ],
        in_specs=[pl.BlockSpec(memory_space=SMEM)] + [whole] * 2,
        out_specs=[whole] * 4,
        compiler_params=pltpu.CompilerParams(vmem_limit_bytes=12 << 20),
        cost_estimate=pl.CostEstimate(flops=1 << 27, bytes_accessed=1 << 20, transcendentals=0),
    )(place, own, other)


def pack_kernel(place, own, other, onehots, below, *outs):
    experts, fan, _ = own.shape
    units = outs[0].shape[0] - below.shape[1]
    for e in range(experts):
        packed = jnp.concatenate([own[e], other[e]], axis=1)
        packed = jnp.dot(packed, onehots[e], preferred_element_type=f32)
        for h in range(fan // units):
            q = e * (fan // units) + h
            part = jnp.concatenate([packed[h * units : (h + 1) * units], below[q]], axis=0)
            part = part.astype(bf16)
            step = lax.rem(q + len(outs) - place[0], len(outs))
            for k, out in enumerate(outs):

                @pl.when(step == k)
                def _(out=out, part=part):
                    out[...] = part


def pack(place, own, other, onehots, below):
    experts, fan, _ = own.shape
    parts, lines, slots = below.shape
    whole = pl.BlockSpec(memory_space=VMEM)
    return pl.pallas_call(
        pack_kernel,
        out_shape=[jax.ShapeDtypeStruct((experts * fan // parts + lines, slots), bf16)] * parts,
        in_specs=[pl.BlockSpec(memory_space=SMEM)] + [whole] * 4,
        out_specs=[whole] * parts,
        compiler_params=pltpu.CompilerParams(vmem_limit_bytes=12 << 20),
        cost_estimate=pl.CostEstimate(flops=1 << 28, bytes_accessed=2 << 20, transcendentals=0),
    )(place, own, other, onehots, below)


def split_kernel(*refs):
    *pieces, rows, features, routes = refs
    width, at = features.shape[1], 0
    for piece in pieces:
        count = piece.shape[0]
        if rows is not None:
            rows[at : at + count] = piece[...]
        features[at : at + count] = piece[:, :width]
        routes[at : at + count] = piece[:, width:]
        at += count


def split(pieces, width, joined):
    count, columns = sum(p.shape[0] for p in pieces), pieces[0].shape[1]
    whole = pl.BlockSpec(memory_space=VMEM)
    widths = [columns] * joined + [width, columns - width]

    def kernel(*refs):
        outs = refs[len(pieces) :]
        split_kernel(*refs[: len(pieces)], outs[0] if joined else None, *outs[-2:])

    return pl.pallas_call(
        kernel,
        out_shape=[jax.ShapeDtypeStruct((count, w), pieces[0].dtype) for w in widths],
        in_specs=[whole] * len(pieces),
        out_specs=[whole] * len(widths),
        compiler_params=pltpu.CompilerParams(vmem_limit_bytes=8 << 20),
        cost_estimate=pl.CostEstimate(flops=1, bytes_accessed=1 << 20, transcendentals=0),
    )(*pieces)


def activate_kernel(*refs):
    *parts, share, hidden = refs
    half = len(parts) // 2
    parts = [[p[...].astype(f32) for p in pair] for pair in zip(parts[:half], parts[half:])]
    units, slots = hidden.shape
    count = len(parts)
    means, devs = [], []
    for part in parts:
        stats = part[0][units:]
        means.append(stats[0:1] + stats[1:2] + stats[2:3])
        devs.append(stats[3:4] + stats[4:5] + stats[5:6])
    mean = sum(means) / count
    var = sum(devs) / (count * PART_WIDTH)
    var = var + sum(jnp.square(m - mean) for m in means) / count
    scale = lax.rsqrt(var + epsilon)
    gains = []
    for part in parts:
        terms = part[1][units:]
        gains += [terms[0:1] + terms[1:2] + terms[2:3], terms[3:4] + terms[4:5] + terms[5:6]]
    columns = jnp.transpose(jnp.concatenate(gains, axis=0)[:, :256])[:units]

    def total(g):
        result = sum(part[g][:units] for part in parts)
        for k in range(count):
            result = result + columns[:, 2 * k + g : 2 * k + g + 1] * (means[k] - mean)
        return result * scale

    gate = total(0)
    hidden[...] = (gate * jax.nn.sigmoid(gate) * total(1) * share[0:1]).astype(bf16)


def activate(parts, share):
    whole = pl.BlockSpec(memory_space=VMEM)
    units, slots = parts[0].shape[0] - EXPERTS, parts[0].shape[1]
    return pl.pallas_call(
        activate_kernel,
        out_shape=jax.ShapeDtypeStruct((units, slots), bf16),
        in_specs=[whole] * (len(parts) + 1),
        out_specs=whole,
        compiler_params=pltpu.CompilerParams(vmem_limit_bytes=8 << 20),
        cost_estimate=pl.CostEstimate(flops=1, bytes_accessed=1 << 20, transcendentals=1),
    )(*parts, share)


def scatter_kernel(place, hidden0, hidden1, hidden2, hidden3, ranks, out):
    parts, slots = out.shape[0], hidden0.shape[1]
    for k, hidden in enumerate((hidden0, hidden1, hidden2, hidden3)):
        at = lax.rem(place[0] + k, parts)
        onehot = chosen(ranks[pl.ds(place[1] + at // 2, 1), :], slots)
        out[at] = jnp.dot(hidden[...], onehot, preferred_element_type=f32).astype(bf16)


def scatter(place, hidden, ranks):
    whole = pl.BlockSpec(memory_space=VMEM)
    return pl.pallas_call(
        scatter_kernel,
        out_shape=jax.ShapeDtypeStruct((4, hidden[0].shape[0], ranks.shape[1]), bf16),
        in_specs=[pl.BlockSpec(memory_space=SMEM)] + [whole] * 5,
        out_specs=whole,
        compiler_params=pltpu.CompilerParams(vmem_limit_bytes=16 << 20),
        cost_estimate=pl.CostEstimate(flops=1 << 28, bytes_accessed=1 << 20, transcendentals=0),
    )(place, *hidden, ranks)


def per_device(
    queries,
    cache_keys,
    stored_values,
    lengths,
    residual_in,
    norm_gain,
    expert_ids,
    expert_scores,
    w_gate,
    w_up,
    w_down,
):
    y, x = lax.axis_index("etp"), lax.axis_index("egrp")
    y_size = lax.axis_size("etp")
    attended = attend(queries, cache_keys, stored_values, lengths)
    place = jnp.stack([y, x * w_gate.shape[0]]).astype(jnp.int32)
    stream, held = finish(place, attended, residual_in, norm_gain, expert_ids.T, expert_scores.T)
    rows, width = stream.shape
    gain = lax.dynamic_slice_in_dim(norm_gain, y * width, width, 0).astype(f32)

    units = w_gate.shape[0] * w_gate.shape[2] // y_size
    down = w_down.reshape(-1, width)

    def project(weight, tokens):
        return jnp.einsum("edf,rd->efr", weight, tokens, preferred_element_type=f32).astype(bf16)

    across = along_z(held, 4)
    chip = jnp.concatenate([held, swap_core(held)], axis=0)
    held = jnp.concatenate([held, across] + [along_z(chip, k) for k in (1, 2, 3)], axis=0)
    gain, held = lax.optimization_barrier((gain, held))
    gains = jnp.stack(
        [jnp.einsum("edf,d->ef", w.astype(f32), gain).reshape(y_size, -1) for w in (w_gate, w_up)]
    )

    terms, rest = [], gains
    for _ in range(3):
        terms.append(lax.reduce_precision(rest, 8, 7))
        rest = rest - terms[-1]
    gains = jnp.stack(terms, axis=1).reshape(2 * len(terms), y_size, units).swapaxes(0, 1)
    slots = 4 * held.shape[0] * 2 * CAPACITY_OF_512 // 512
    gains = jnp.pad(gains, ((0, 0), (0, EXPERTS - gains.shape[1]), (0, slots - units)))
    pieces = [along_x(held, k) for k in range(3)]
    pieces, gains = lax.optimization_barrier((pieces, gains))
    own, own_rows, own_notes = split([held] + pieces, width, True)
    other_rows, other_notes = split([swap_core(own)], width, False)
    onehots, stats, share, ranks = list_rows(
        place, own_notes, other_notes, w_gate.shape[0], y_size
    )
    gate_sums = [project(w_gate, r) for r in (own_rows, other_rows)]
    gate_parts = pack(place, *gate_sums, onehots, stats)
    own_rows, other_rows, gate_parts = lax.optimization_barrier((own_rows, other_rows, gate_parts))
    up_sums = [project(w_up, r) for r in (own_rows, other_rows)]
    up_parts = pack(place, *up_sums, onehots, gains)
    parts = []
    for packed in (gate_parts, up_parts):
        parts += [packed[0]] + [to_y(packed[k], k) for k in range(1, y_size)]
    hidden = activate(parts, share)
    got = {k: to_y(hidden, -k) for k in (1, 3, 2)}
    hidden = scatter(place, [hidden] + [got[k] for k in range(1, y_size)], ranks)
    hidden = hidden.reshape(down.shape[0], -1)
    n = own.shape[0] // 4

    def over_cores(hidden, first, last):
        def output(at):
            part = hidden[:, at + first * n : at + last * n]
            return jnp.einsum("fr,fd->rd", part, down, preferred_element_type=f32)

        other = swap_core(output(4 * n).astype(bf16))
        return lax.optimization_barrier(output(0)) + other.astype(f32)

    distant = over_cores(hidden, 3, 4).astype(bf16)
    distant, hidden = lax.optimization_barrier((distant, hidden))
    total = over_cores(hidden, 0, 3)
    total, *sent = lax.optimization_barrier(
        (total[:n], total[n : 2 * n].astype(bf16), total[2 * n :].astype(bf16))
    )
    got = [along_x(part, k) for k, part in enumerate(sent + [distant])]
    total = total + sum(part.astype(f32) for part in got)
    n = 2 * rows
    mine, across, *chip = lax.optimization_barrier(
        (total[:rows], total[rows:n].astype(bf16))
        + tuple(total[k * n : (k + 1) * n].astype(bf16) for k in (1, 2, 3))
    )
    chip = sum(along_z(part, k + 1, True).astype(f32) for k, part in enumerate(chip))
    mine = mine + along_z(across, 4, True).astype(f32) + chip[:rows]
    mine = mine + swap_core(chip[rows:].astype(bf16)).astype(f32)
    return (stream, mine.astype(bf16))


def solution(mesh):
    placed = (
        P(("attn", "egrp"), "etp"),
        P(("attn", "egrp"), None, "etp"),
        P(("attn", "egrp"), None, "etp"),
        P(("attn", "egrp")),
        P(("attn", "egrp"), "etp"),
        P(),
        P(("attn", "egrp"), None),
        P(("attn", "egrp"), None),
        P("egrp", "etp", "attn"),
        P("egrp", "etp", "attn"),
        P("egrp", "attn", "etp"),
    )
    return jax.shard_map(
        per_device,
        mesh=mesh,
        in_specs=placed,
        out_specs=(P(("attn", "egrp"), "etp"), P(("attn", "egrp"), "etp")),
        check_vma=False,
    )
```
